128 devices in a mesh: mesh: 32 (over y, z, core), comp: 4 (over x).
Axes of the slice: x: 4, y: 4, z: 4, core: 2. Of those that a mesh axis runs over, the one named last changes fastest.
Arguments:
- a_blocks: bfloat16 [6144, 64, 448], P(('mesh', 'comp')), may hold values from -0.25 to 0.25
- a_columns: int32 [6144, 7], P(('mesh', 'comp')), may hold values from 0 to 71, as said below
- p_blocks: bfloat16 [6144, 64, 192], P(('mesh', 'comp')), may hold values from -0.75 to 0.75
- p_columns: int32 [6144, 3], P(('mesh', 'comp')), may hold values from 0 to 3, all different within a row
- r_blocks: bfloat16 [6144, 64, 192], P(('mesh', 'comp')), may hold values from -0.75 to 0.75
- r_columns: int32 [6144, 3], P(('mesh', 'comp')), may hold values from 0 to 11, as said below
- sent_up: int32 [1536], P(('mesh', 'comp')), may hold values from 0 to 47, as said below
- sent_down: int32 [1536], P(('mesh', 'comp')), may hold values from 0 to 47, as said below
- vectors: bfloat16 [6144, 128], P(('mesh', 'comp')), may hold values from -2 to 2
- coarse_dest: int32 [512, 1], P(('mesh', 'comp')), may hold values from 0 to 3; in each aligned block of 4 rows (0 to 3, 4 to 7, ...) at most 2 rows name the same one
Outputs:
- coarse_matrix: bfloat16 [1024, 64, 1280], P(('mesh', 'comp'))
- coarse_vectors: bfloat16 [1024, 128], P(('mesh', 'comp'))
The draws below stay inside these ranges and needn't reach their ends.
Inputs may be any that keep to these rules, and one draw needn't show every extreme that they name: `a_columns`: each fine row's first column is the row itself (its own local number). A column 48 + i exists only on devices with a device below along mesh, 60 + i only on devices with one above; every listed ghost of an existing neighbour is named by some row. `r_columns`: h is never toward a device missing along mesh. Local row numbers; the 12 entries of one device in sent_up and in sent_down are distinct, and no row is in both lists. `sent_down`: see sent_up. `coarse_dest`: at most 2 of the 4 coarse rows of one home go to one owner comp, and that many do in some home. `p_columns`: the 3 entries of a row are distinct.
All inputs are finite; a program needn't handle non-finite values.
Results may differ from the reference program's by a relative error of at most 0.0049.
Values may be sent and summed in bfloat16 or wider, within the bound.
No kernel may reach another device: no remote copies, remote signals or barrier semaphores. Data moves between devices by JAX's collectives and lax.ppermute only.
A program may use at most 128 MiB of HBM per device.

```python
import math
import jax
import jax.numpy as jnp
import numpy as np
from jax import lax

B = 64
KA = 7
KP = 3
KR = 3
NB = 48
NCL = 4
GH = 12
CAP = 2
W = 20
NF = 6144
NC = 512
OWN_SLOTS = 1024
N_MESH = 32
N_COMP = 4
DEVICES = 128


def ghost_orders(key):
    keys = jax.random.split(key, DEVICES)
    return jax.vmap(lambda single: jax.random.permutation(single, NB))(keys).astype(jnp.int32)


def draw_sent_up(key, part):
    orders = ghost_orders(key)
    return orders[:, :GH].reshape(DEVICES * GH)


def draw_sent_down(key, part):
    orders = ghost_orders(key)
    return orders[:, GH:2 * GH].reshape(DEVICES * GH)


def draw_a_columns(key, part):
    key = jax.random.fold_in(key, 11)
    first_key, second_key, third_key, fourth_key = jax.random.split(key, 4)
    local = jax.random.randint(first_key, (DEVICES, NB, KA), 0, NB).astype(jnp.int32)
    local = local.at[:, :, 0].set(jnp.arange(NB, dtype=jnp.int32)[None, :])
    orders = jax.vmap(lambda single: jax.random.permutation(single, NB))(jax.random.split(second_key, DEVICES)).astype(jnp.int32)
    mesh_pos = jnp.arange(DEVICES, dtype=jnp.int32) // N_COMP
    choose_ghost = jax.random.randint(third_key, (DEVICES, NB, KA), 0, 6)
    ghost_pick = jax.random.randint(fourth_key, (DEVICES, NB, KA), 0, 2 * GH)
    allowed = jnp.where(ghost_pick < GH, mesh_pos[:, None, None] > 0, mesh_pos[:, None, None] < N_MESH - 1)
    later = jnp.arange(KA, dtype=jnp.int32)[None, None, :] >= 3
    local = jnp.where((choose_ghost == 0) & later & allowed, NB + ghost_pick, local).astype(jnp.int32)
    ghost_index = jnp.arange(GH, dtype=jnp.int32)

    def one_device(rows, order, position):
        low_rows = order[:GH]
        high_rows = order[GH:2 * GH]
        low_values = jnp.where(position > 0, NB + ghost_index, rows[low_rows, 1])
        high_values = jnp.where(position < N_MESH - 1, NB + GH + ghost_index, rows[high_rows, 2])
        rows = rows.at[low_rows, 1].set(low_values)
        return rows.at[high_rows, 2].set(high_values)
    return jax.vmap(one_device)(local, orders, mesh_pos).reshape(NF, KA).astype(jnp.int32)


def draw_r_columns(key, part):
    key = jax.random.fold_in(key, 31)
    first_key, second_key = jax.random.split(key)
    side = jax.random.randint(first_key, (DEVICES, NB, KR), 0, 3).astype(jnp.int32)
    mesh_pos = (jnp.arange(DEVICES, dtype=jnp.int32) // N_COMP)[:, None, None]
    side = jnp.where((mesh_pos == 0) & (side == 0), 1, side)
    side = jnp.where((mesh_pos == N_MESH - 1) & (side == 2), 1, side)
    within = jax.random.randint(second_key, (DEVICES, NB, KR), 0, NCL).astype(jnp.int32)
    return (side * NCL + within).reshape(NF, KR).astype(jnp.int32)


def steps_of(rng, dims, cuts, smallest, top_value):
    factor_of = 1.0
    for axis_at, parts in cuts:
        steps = jax.random.uniform(jax.random.fold_in(jax.random.fold_in(rng, 6), axis_at), (parts,), jnp.float32, smallest / len(cuts), top_value / len(cuts))
        factor_of = factor_of * jnp.repeat(jnp.exp(steps), dims[axis_at] // parts).reshape((-1,) + (1,) * (len(dims) - 1 - axis_at))
    return factor_of


def different_ones(stream_key, rows, amount, top, lift):
    order = jax.random.permutation(jax.random.fold_in(stream_key, 1), amount)
    boost = order
    for power in range(3):
        boost = boost * boost // amount
    boost = boost * lift // amount
    chance = jax.random.randint(jax.random.fold_in(stream_key, 2), (rows, amount), 0, 4096) + boost
    fixed_rows = jax.random.permutation(jax.random.fold_in(stream_key, 3), rows)[jnp.arange(amount) % rows]
    chance = jnp.where(jnp.arange(rows)[:, None] == fixed_rows[None, :], 1 << 14, chance)
    merit = chance * amount + jnp.arange(amount)
    return lax.top_k(merit.astype(jnp.int32), top)[1].astype(jnp.int32)


def shared_out(key, own, number, rows, number_of, top, reach, slope):
    order = jax.random.permutation(key, number_of)
    heavy_load, ordinary = load_shares(number_of, rows * top, reach, slope, True), load_shares(number_of, rows * top, reach, slope, False)
    places = jnp.arange(number_of)

    def named(lengths, offset_by):
        used = int((lengths > 0).sum())
        fixed = max(1, used // 4)
        shifted = fixed + (places - fixed + offset_by * (used - fixed)) % max(1, number_of - fixed)
        return jnp.zeros((number_of,), jnp.int32).at[order[jnp.where(places < fixed, places, shifted)]].set(jnp.asarray(lengths, jnp.int32))

    lengths = jnp.where(number % 4 == 0, named(heavy_load, number // 4), named(ordinary, number - number // 4 - 1))
    mixed = jax.random.permutation(jax.random.fold_in(own, 3), number_of)
    source_of, receiver = mixed[0:number_of // 2 * 2:2], mixed[1:number_of // 2 * 2:2]
    slack = jnp.minimum(lengths[source_of] - 1, reach - lengths[receiver]) // 2
    slack = jnp.where((source_of == order[0]) | (receiver == order[0]) | (lengths[receiver] == 0), 0, jnp.maximum(slack, 0))
    shifted = jax.random.randint(jax.random.fold_in(own, 4), (number_of // 2,), 0, 1 << 20) % (slack + 1)
    lengths = lengths.at[source_of].add(-shifted).at[receiver].add(shifted)
    labels = jnp.searchsorted(jnp.cumsum(lengths), jnp.arange(rows * top), side="right").astype(jnp.int32)
    table = labels.reshape(top, rows).T
    table = table[jax.random.permutation(jax.random.fold_in(own, 1), rows)]
    offset_by = jax.random.randint(jax.random.fold_in(own, 2), (rows, 1), 0, top)
    return jnp.take_along_axis(table, (jnp.arange(top)[None, :] + offset_by) % top, axis=1)


def load_shares(number_of, total, bound, slope, full):
    portions = [(1 << 20) // math.isqrt(rank ** slope) + 1 for rank in range(1, number_of + 1)]
    largest = bound if full else min(bound, max(-(-total // number_of), total * portions[0] // sum(portions)))
    least = 1 if total - largest >= number_of - 1 else 0
    given, rest = [largest] + [least] * (number_of - 1), total - largest - least * (number_of - 1)
    while rest > 0:
        free = [i for i in range(1, number_of) if given[i] < largest] or [i for i in range(1, number_of) if given[i] < bound]
        pool, remaining = sum([portions[i] for i in free]), rest
        for i in free:
            extra = min(bound - given[i], max(1, remaining * portions[i] // pool), rest)
            given[i] = given[i] + extra
            rest = rest - extra
    return np.array(given)


def noise(key, shape, width, bound, cuts=(), kind=jnp.bfloat16):
    level = steps_of(key, shape, cuts, -0.22, 0.18) if cuts else 1.0
    array = jax.random.normal(key, shape, jnp.float32) * width * level
    return jnp.minimum(jnp.maximum(array, -bound), bound).astype(kind)


def setup_inputs(seed: int = 0) -> dict:
    splits = jax.random.split(jax.random.key(seed), 11)
    a_blocks = noise(splits[0], (NF, B, KA * B), (KA * B) ** -0.5, 0.25, ((0, 128),))
    a_columns = draw_a_columns(jax.random.fold_in(splits[10], 71), 0)
    p_blocks = noise(splits[2], (NF, B, KP * B), B ** -0.5, 0.75, ((0, 128),))
    p_columns = different_ones(splits[3], NF, NCL, KP, 0)
    r_blocks = noise(splits[4], (NF, B, KR * B), B ** -0.5, 0.75, ((0, 128),))
    r_columns = draw_r_columns(jax.random.fold_in(splits[10], 71), 0)
    sent_up = draw_sent_up(jax.random.fold_in(splits[10], 71), 0)
    sent_down = draw_sent_down(jax.random.fold_in(splits[10], 71), 0)
    vectors = noise(splits[8], (NF, 2 * B), 0.25, 2.0, ((0, 128),))
    coarse_dest_keys = jax.random.split(jax.random.fold_in(splits[9], 1), NC // NCL)
    coarse_dest_turns = jax.random.permutation(jax.random.fold_in(splits[9], 3), NC // NCL)
    coarse_dest = jax.vmap(lambda own, number: shared_out(jax.random.fold_in(splits[9], 2), own, number, NCL, N_COMP, 1, CAP, 1))(coarse_dest_keys, coarse_dest_turns).reshape((NC, 1))
    return dict(a_blocks=a_blocks, a_columns=a_columns, p_blocks=p_blocks, p_columns=p_columns, r_blocks=r_blocks, r_columns=r_columns, sent_up=sent_up, sent_down=sent_down, vectors=vectors, coarse_dest=coarse_dest)


def densify(values, columns):
    count = values.shape[0]
    blocks = values.astype(jnp.float32).reshape(count, B, KP, B)
    onehot = (columns[:, :, None] == jnp.arange(NCL, dtype=jnp.int32)[None, None, :]).astype(jnp.float32)
    return jnp.einsum('rqs,rbqc->rbsc', onehot, blocks).reshape(count, B, NCL * B)


def widen(strip, offset):
    seg_width = NCL * B
    return jnp.pad(strip, ((0, 0), (0, 0), ((1 - offset) * seg_width, (1 + offset) * seg_width)))


def reference(a_blocks, a_columns, p_blocks, p_columns, r_blocks, r_columns, sent_up, sent_down, vectors, coarse_dest):
    def device_terms(device):
        mesh_pos = device // N_COMP
        lower = jnp.maximum(device - N_COMP, 0).astype(jnp.int32)
        upper = jnp.minimum(device + N_COMP, DEVICES - 1).astype(jnp.int32)
        first = (device * NB).astype(jnp.int32)
        a_rows = lax.dynamic_slice_in_dim(a_blocks, first, NB, 0).astype(jnp.float32)
        columns = lax.dynamic_slice_in_dim(a_columns, first, NB, 0)
        own_rows = densify(lax.dynamic_slice_in_dim(p_blocks, first, NB, 0), lax.dynamic_slice_in_dim(p_columns, first, NB, 0))
        low_ids = (lower * NB + lax.dynamic_slice_in_dim(sent_up, (lower * GH).astype(jnp.int32), GH, 0)).astype(jnp.int32)
        high_ids = (upper * NB + lax.dynamic_slice_in_dim(sent_down, (upper * GH).astype(jnp.int32), GH, 0)).astype(jnp.int32)
        low_rows = densify(p_blocks[low_ids], p_columns[low_ids]) * (mesh_pos > 0).astype(jnp.float32)
        high_rows = densify(p_blocks[high_ids], p_columns[high_ids]) * (mesh_pos < N_MESH - 1).astype(jnp.float32)
        p_table = jnp.concatenate([own_rows, low_rows, high_rows], 0)
        segment = jnp.where(columns < NB, 1, jnp.where(columns < NB + GH, 0, 2)).astype(jnp.int32)
        applied = jnp.zeros((NB, B, 3, NCL * B), jnp.float32)
        for k in range(KA):
            product = jnp.einsum('fab,fbc->fac', a_rows[:, :, k * B:(k + 1) * B], p_table[columns[:, k]])
            chooser = (segment[:, k][:, None] == jnp.arange(3, dtype=jnp.int32)[None, :]).astype(jnp.float32)
            applied = applied + product[:, :, None, :] * chooser[:, None, :, None]
        applied = applied.reshape(NB, B, 3 * NCL * B).astype(jnp.bfloat16)
        applied = lax.optimization_barrier(applied).astype(jnp.float32)
        r_rows = lax.dynamic_slice_in_dim(r_blocks, first, NB, 0).astype(jnp.float32)
        targets = lax.dynamic_slice_in_dim(r_columns, first, NB, 0)
        vec_rows = lax.dynamic_slice_in_dim(vectors, first, NB, 0).astype(jnp.float32).reshape(NB, 2, B)
        terms = jnp.zeros((3 * NCL, B, 3 * NCL * B), jnp.float32)
        vec_terms = jnp.zeros((3 * NCL, 2, B), jnp.float32)
        for j in range(KR):
            r_block = r_rows[:, :, j * B:(j + 1) * B]
            terms = terms.at[targets[:, j]].add(jnp.einsum('fab,fbx->fax', r_block, applied))
            vec_terms = vec_terms.at[targets[:, j]].add(jnp.einsum('fab,ftb->fta', r_block, vec_rows))
        return terms, vec_terms

    def accumulate(device, carry):
        coarse_sum, vec_sum = carry
        terms, vec_terms = device_terms(device)
        for offset in (-1, 0, 1):
            home = device + offset * N_COMP
            valid = ((home >= 0) & (home < DEVICES)).astype(jnp.float32)
            start = (jnp.clip(home, 0, DEVICES - 1) * NCL).astype(jnp.int32)
            piece = widen(terms[(offset + 1) * NCL:(offset + 2) * NCL], offset) * valid
            vec_piece = vec_terms[(offset + 1) * NCL:(offset + 2) * NCL] * valid
            current = lax.dynamic_slice_in_dim(coarse_sum, start, NCL, 0)
            coarse_sum = lax.dynamic_update_slice_in_dim(coarse_sum, current + piece, start, 0)
            vec_now = lax.dynamic_slice_in_dim(vec_sum, start, NCL, 0)
            vec_sum = lax.dynamic_update_slice_in_dim(vec_sum, vec_now + vec_piece, start, 0)
        return coarse_sum, vec_sum

    initial = (jnp.zeros((NC, B, W * B), jnp.float32), jnp.zeros((NC, 2, B), jnp.float32))
    coarse_sum, vec_sum = lax.fori_loop(jnp.int32(0), jnp.int32(DEVICES), accumulate, initial)
    home_of = jnp.arange(NC, dtype=jnp.int32) // NCL
    owner = coarse_dest[:, 0]
    onehot = (owner.reshape(DEVICES, NCL)[:, :, None] == jnp.arange(N_COMP, dtype=jnp.int32)[None, None, :]).astype(jnp.int32)
    ranking = jnp.sum((jnp.cumsum(onehot, 1).astype(jnp.int32) - onehot) * onehot, 2).astype(jnp.int32).reshape(NC)
    slots = ((((home_of // N_COMP) * N_COMP + owner) * N_COMP + home_of % N_COMP) * CAP + ranking).astype(jnp.int32)
    coarse_matrix = jnp.zeros((OWN_SLOTS, B, W * B), jnp.bfloat16).at[slots].set(coarse_sum.astype(jnp.bfloat16))
    coarse_vectors = jnp.zeros((OWN_SLOTS, 2 * B), jnp.bfloat16).at[slots].set(vec_sum.reshape(NC, 2 * B).astype(jnp.bfloat16))
    return coarse_matrix, coarse_vectors
```

```python
import functools

import jax
import jax.numpy as jnp
from jax import lax
from jax.experimental import pallas as pl
from jax.experimental.pallas import tpu as pltpu
from jax.sharding import PartitionSpec as P

BF = jnp.bfloat16
F32 = jnp.float32
MIB = 1 << 20


def params(mib=48):
    return pltpu.CompilerParams(vmem_limit_bytes=mib * MIB)


VM = pl.BlockSpec(memory_space=pltpu.VMEM)
SM = pl.BlockSpec(memory_space=pltpu.SMEM)
ANY = pl.BlockSpec(memory_space=pl.ANY)


def half_of_lane():
    return (lax.broadcasted_iota(jnp.int32, (16, 128), 1) >= 64).astype(jnp.int32)


def dense_row(x, cols, half, coarse):
    width = x.shape[0]
    tiles = []
    doubled = []
    for q in range(len(cols)):
        block = x[:, q * width : (q + 1) * width]
        doubled.append(jnp.concatenate([block, block], 1).reshape(width // 16, 16, 2 * width))
    for t in range(coarse // 2):
        total = None
        for q in range(len(cols)):
            mask = jnp.where(half == cols[q] - 2 * t, 1.0, 0.0).astype(BF)
            term = doubled[q] * mask[None]
            total = term if total is None else total + term
        tiles.append(total.reshape(width, 2 * width))
    return tiles


def send_kernel(pcol, up, down, par, p_ref, out_a, out_b, *, coarse):
    width = p_ref.shape[1]
    half = half_of_lane()
    even = par[0] == 0
    for i in range(up.shape[0]):
        for out, first, second in ((out_b, down, up), (out_a, up, down)):
            f = jnp.where(even, first[i], second[i])
            cols = [pcol[q, f] for q in range(pcol.shape[0])]
            tiles = dense_row(p_ref[f], cols, half, coarse)
            for t, tile in enumerate(tiles):
                out[i * width : (i + 1) * width, t * 128 : (t + 1) * 128] = tile


def own_kernel(
    acol, pcol, rcol, a_hbm, p_hbm, r_hbm, v_ref, ap_out, rd_out, a_v, p_v, r_v, table, sems, *, coarse
):
    rows, width = a_v.shape[0], a_v.shape[1]
    kas, krs = acol.shape[0], rcol.shape[0]
    copies = [
        pltpu.make_async_copy(p_hbm, p_v, sems.at[0]),
        pltpu.make_async_copy(r_hbm, r_v, sems.at[1]),
        pltpu.make_async_copy(a_hbm, a_v, sems.at[2]),
    ]
    for copy in copies:
        copy.start()
    half = half_of_lane()
    table[rows * width :, :] = jnp.zeros((width, coarse * width), BF)
    copies[0].wait()

    def densify(f, _):
        cols = [pcol[q, f] for q in range(pcol.shape[0])]
        at = pl.ds(pl.multiple_of(f * width, width), width)
        for t, tile in enumerate(dense_row(p_v[f], cols, half, coarse)):
            table[at, t * 128 : (t + 1) * 128] = tile
        return 0

    lax.fori_loop(0, rows, densify, 0, unroll=4)
    copies[1].wait()
    right = lax.broadcasted_iota(jnp.int32, (width, 128), 1) >= width
    for pair in range(rows // 2):
        lanes = slice(pair * 128, (pair + 1) * 128)
        one, other = r_v[2 * pair], r_v[2 * pair + 1]
        blocks, names = [], []
        for j in range(krs):
            cut = slice(j * width, (j + 1) * width)
            blocks.append(jnp.concatenate([one[:, cut], other[:, cut]], 1))
            names.append(jnp.where(right, rcol[j, 2 * pair + 1], rcol[j, 2 * pair]).astype(F32).astype(BF))
        for s in range(3 * coarse):
            total = None
            for block, name in zip(blocks, names):
                term = jnp.where(name == jnp.asarray(s, BF), block, jnp.zeros_like(block))
                total = term if total is None else total + term
            rd_out[s * width : (s + 1) * width, lanes] = total
    copies[2].wait()

    def apply(f, _):
        picked = []
        for k in range(kas):
            c = acol[k, f]
            c = jnp.where(c < rows, c, rows)
            picked.append(table[pl.ds(pl.multiple_of(c * width, width), width), :])
        strip = jnp.dot(a_v[f], jnp.concatenate(picked, 0), preferred_element_type=F32)
        ap_out[pl.ds(pl.multiple_of(f * width, width), width), :] = strip.astype(BF)
        return 0

    lax.fori_loop(0, rows, apply, 0, unroll=8)


def ghost_kernel(
    acol, par, got_a, got_b, a_hbm, rd_ref, ap_ref, v_ref, send_a, send_b, own, own_vec,
    a_v, table, strips, sems, *, coarse
):
    rows, width = a_v.shape[0], a_v.shape[1]
    kas = acol.shape[0]
    ghosts = got_a.shape[0] // width
    seg = coarse * width
    block = ghosts * width
    copy = pltpu.make_async_copy(a_hbm, a_v, sems.at[0])
    copy.start()
    odd = par[0]
    table[pl.ds(pl.multiple_of((1 - odd) * block, block), block), :] = got_a[...]
    table[pl.ds(pl.multiple_of(odd * block, block), block), :] = got_b[...]
    table[2 * block :, :] = jnp.zeros((width, seg), BF)
    strips[:, seg : 2 * seg] = ap_ref[...]

    flat = jnp.concatenate([v_ref[...].astype(F32), jnp.zeros((128 - rows, 2 * width), F32)], 0)
    turned = flat.T
    lane = lax.broadcasted_iota(jnp.int32, (width, 128), 1)
    both = jnp.where(lane < width, turned[:width], pltpu.roll(turned[width:], width, 1))
    at_lane = lane % width
    for f in range(rows):
        strips[f * width : (f + 1) * width, 3 * seg :] = jnp.where(at_lane == f, both, 0.0).astype(BF)
    copy.wait()

    def apply(f, _):
        at = pl.ds(pl.multiple_of(f * width, width), width)
        cols = [acol[k, f] - rows for k in range(kas)]
        for side in (0, 1):
            picked = []
            for k in range(kas):
                c = cols[k]
                inside = (c >= side * ghosts) & (c < (side + 1) * ghosts)
                c = jnp.where(inside, c, 2 * ghosts)
                picked.append(table[pl.ds(pl.multiple_of(c * width, width), width), :])
            strip = jnp.dot(a_v[f], jnp.concatenate(picked, 0), preferred_element_type=F32)
            strips[at, side * 2 * seg : (side * 2 + 1) * seg] = strip.astype(BF)
        return 0

    lax.fori_loop(0, rows, apply, 0, unroll=4)

    def restrict(start, out, out_vec, kind):
        r = rd_ref[pl.ds(pl.multiple_of(start, seg), seg), :]
        for e in range(3):
            lanes = slice(e * seg, (e + 1) * seg)
            out[0:seg, lanes] = jnp.dot(r, strips[:, lanes], preferred_element_type=F32).astype(kind)
        spread = jnp.dot(r, strips[:, 3 * seg :], preferred_element_type=F32)
        pieces = []
        for n in range(seg // 128):
            t = spread[n * 128 : (n + 1) * 128].T
            pieces.append(jnp.concatenate(
                [jnp.sum(t[i * width : (i + 1) * width], 0, keepdims=True) for i in range(2)], 0))
        vec = jnp.concatenate(pieces, 1)
        vec = jnp.concatenate([vec, jnp.zeros((14, seg), F32)], 0).astype(kind)
        if out_vec is None:
            out[seg : seg + 16, 0:seg] = vec
            out[seg : seg + 16, seg:] = jnp.zeros((16, 2 * seg), kind)
        else:
            out_vec[...] = vec

    restrict(seg * 2 * (1 - odd), send_a, None, BF)
    restrict(seg * 2 * odd, send_b, None, BF)
    restrict(seg, own, own_vec, F32)


def sum_kernel(dest, par, comp, got_a, got_b, own, own_vec, *outs, coarse):
    seg = own.shape[0]
    width = seg // coarse
    odd = par[0] == 1
    owners = [dest[0, s] for s in range(coarse)]
    ranks = []
    for s in range(coarse):
        rank = jnp.int32(0)
        for earlier in range(s):
            rank = rank + (owners[earlier] == owners[s]).astype(jnp.int32)
        ranks.append(rank)
    away = [lax.rem(owners[s] - comp[0] + 4, 4) for s in range(coarse)]
    low_vec = jnp.where(odd, got_a[seg : seg + 16, 0:seg].astype(F32), got_b[seg : seg + 16, 0:seg].astype(F32))
    high_vec = jnp.where(odd, got_b[seg : seg + 16, 0:seg].astype(F32), got_a[seg : seg + 16, 0:seg].astype(F32))
    vec = own_vec[...] + low_vec + high_vec
    lines = []
    for s in range(coarse):
        lines.append(jnp.concatenate(
            [vec[0:1, s * width : (s + 1) * width], vec[1:2, s * width : (s + 1) * width]], 1))
    row = lax.broadcasted_iota(jnp.int32, (16, 128), 0)
    for distance, out in enumerate(outs):
        block = jnp.zeros((16, 128), F32)
        for s in range(coarse):
            hit = jnp.where(away[s] == distance, ranks[s], -1)
            block = block + jnp.where(row == hit, lines[s], 0.0)
        out[2 * width :, 0:128] = block.astype(BF)
        out[2 * width :, 128:] = jnp.zeros((16, 5 * seg - 128), BF)
        for k in range(2):
            source = jnp.int32(-1)
            for s in range(coarse):
                source = jnp.where((away[s] == distance) & (ranks[s] == k), s, source)
            into = slice(k * width, (k + 1) * width)

            def fill(below, above, out=out, into=into, source=source):
                at = pl.ds(pl.multiple_of(jnp.maximum(source, 0) * width, width), width)
                for u in range(5):
                    total = None
                    for ref, first in ((own, 1), (below, 0), (above, 2)):
                        e = u - first
                        if 0 <= e < 3:
                            term = ref[at, e * seg : (e + 1) * seg].astype(F32)
                            total = term if total is None else total + term
                    out[into, u * seg : (u + 1) * seg] = total.astype(BF)

            @pl.when((source >= 0) & odd)
            def _():
                fill(got_a, got_b)

            @pl.when((source >= 0) & jnp.logical_not(odd))
            def _():
                fill(got_b, got_a)

            @pl.when(source < 0)
            def _():
                out[into, :] = jnp.zeros((width, 5 * seg), BF)


def gather_kernel(comp, *refs):
    parts, matrix, vectors = refs[:4], refs[4], refs[5]
    width = matrix.shape[1]
    row = lax.broadcasted_iota(jnp.int32, (8, 128), 0)
    total = jnp.zeros((8, 128), F32)
    for distance, part in enumerate(parts):
        source = lax.rem(comp[0] - distance + 4, 4)
        for k in range(2):
            matrix[source * 2 + k] = part[k * width : (k + 1) * width, :]
            line = part[2 * width :, 0:128].astype(F32)[k : k + 1]
            total = total + jnp.where(row == source * 2 + k, line, 0.0)
    vectors[...] = total.astype(BF)


def exchange(block_a, block_b):
    n = lax.axis_size("mesh")
    within = [(i, i ^ 1) for i in range(n)]
    across = [(i, i + 1 if i % 2 else i - 1) for i in range(1, n - 1)]
    got_b = lax.ppermute(block_b, "mesh", across)
    got_a = lax.ppermute(block_a, "mesh", within)
    return got_a, got_b


def on_device(a_blocks, a_columns, p_blocks, p_columns, r_blocks, r_columns, sent_up, sent_down, vectors, coarse_dest):
    rows, width = a_blocks.shape[0], a_blocks.shape[1]
    ghosts = sent_up.shape[0]
    coarse = coarse_dest.shape[0]
    seg = coarse * width
    acol, pcol, rcol, dest = a_columns.T, p_columns.T, r_columns.T, coarse_dest.T
    par = (lax.axis_index("mesh") % 2).astype(jnp.int32).reshape(1)
    comp = lax.axis_index("comp").astype(jnp.int32).reshape(1)
    shape = jax.ShapeDtypeStruct
    out_a, out_b = pl.pallas_call(
        functools.partial(send_kernel, coarse=coarse),
        out_shape=[shape((ghosts * width, seg), BF)] * 2,
        in_specs=[SM, SM, SM, SM, VM],
        out_specs=[VM, VM],
        compiler_params=params(),
        name="send_rows",
    )(pcol, sent_up, sent_down, par, p_blocks)
    got_a, got_b = exchange(out_a, out_b)
    strips, r_dense = pl.pallas_call(
        functools.partial(own_kernel, coarse=coarse),
        out_shape=[shape((rows * width, seg), BF), shape((3 * seg, rows * width), BF)],
        in_specs=[SM, SM, SM, ANY, ANY, ANY, VM],
        out_specs=[VM, VM],
        scratch_shapes=[
            pltpu.VMEM(a_blocks.shape, BF),
            pltpu.VMEM(p_blocks.shape, BF),
            pltpu.VMEM(r_blocks.shape, BF),
            pltpu.VMEM(((rows + 1) * width, seg), BF),
            pltpu.SemaphoreType.DMA((3,)),
        ],
        compiler_params=params(),
        cost_estimate=pl.CostEstimate(flops=4 * 10**9, bytes_accessed=20 * 10**6, transcendentals=0),
        name="own_columns",
    )(acol, pcol, rcol, a_blocks, p_blocks, r_blocks, vectors)
    send_a, send_b, own, own_vec = pl.pallas_call(
        functools.partial(ghost_kernel, coarse=coarse),
        out_shape=[shape((seg + 16, 3 * seg), BF)] * 2 + [shape((seg, 3 * seg), F32), shape((16, seg), F32)],
        in_specs=[SM, SM, VM, VM, ANY, VM, VM, VM],
        out_specs=[VM] * 4,
        scratch_shapes=[
            pltpu.VMEM(a_blocks.shape, BF),
            pltpu.VMEM(((2 * ghosts + 1) * width, seg), BF),
            pltpu.VMEM((rows * width, 3 * seg + 128), BF),
            pltpu.SemaphoreType.DMA((1,)),
        ],
        compiler_params=params(),
        name="ghost_columns",
    )(acol, par, got_a, got_b, a_blocks, r_dense, strips, vectors)
    from_a, from_b = exchange(send_a, send_b)
    outs = pl.pallas_call(
        functools.partial(sum_kernel, coarse=coarse),
        out_shape=[shape((2 * width + 16, 5 * seg), BF)] * 4,
        in_specs=[SM, SM, SM, VM, VM, VM, VM],
        out_specs=[VM] * 4,
        compiler_params=params(),
        name="sum_rows",
    )(dest, par, comp, from_a, from_b, own, own_vec)
    parts = [outs[0]]
    turned = {}
    for distance in (2, 1, 3):
        turned[distance] = lax.ppermute(outs[distance], "comp", [(i, (i + distance) % 4) for i in range(4)])
    return pl.pallas_call(
        gather_kernel,
        out_shape=[shape((8, width, 5 * seg), BF), shape((8, 2 * width), BF)],
        in_specs=[SM] + [VM] * 4,
        out_specs=[VM, VM],
        compiler_params=params(),
        name="into_slots",
    )(comp, outs[0], turned[1], turned[2], turned[3])


def solution(mesh):
    placed = (
        P(("mesh", "comp"), None, None),
        P(("mesh", "comp"), None),
        P(("mesh", "comp"), None, None),
        P(("mesh", "comp"), None),
        P(("mesh", "comp"), None, None),
        P(("mesh", "comp"), None),
        P(("mesh", "comp")),
        P(("mesh", "comp")),
        P(("mesh", "comp"), None),
        P(("mesh", "comp"), None),
    )
    return jax.shard_map(
        on_device,
        mesh=mesh,
        in_specs=placed,
        out_specs=(P(("mesh", "comp"), None, None), P(("mesh", "comp"), None)),
        check_vma=False,
    )
```

```python
import functools

import jax
import jax.numpy as jnp
from jax import lax
from jax.experimental import pallas as pl
from jax.experimental.pallas import tpu as pltpu
from jax.sharding import PartitionSpec as P

BF = jnp.bfloat16
F32 = jnp.float32
MIB = 1 << 20
K1_MIB = 54
K1_FLOPS = 20 * 10**9
K2_MIB = 24
HS = [slice(0, 768)]


def params(mib=24):
    return pltpu.CompilerParams(vmem_limit_bytes=mib * MIB)


VM = pl.BlockSpec(memory_space=pltpu.VMEM)
SM = pl.BlockSpec(memory_space=pltpu.SMEM)
ANY = pl.BlockSpec(memory_space=pl.ANY)


def half_of_lane():
    return (lax.broadcasted_iota(jnp.int32, (16, 128), 1) >= 64).astype(jnp.int32)


def dense_row(x, cols, half, coarse):
    width = x.shape[0]
    tiles = []
    doubled = []
    for q in range(len(cols)):
        block = x[:, q * width : (q + 1) * width]
        doubled.append(jnp.concatenate([block, block], 1).reshape(width // 16, 16, 2 * width))
    for t in range(coarse // 2):
        total = None
        for q in range(len(cols)):
            mask = jnp.where(half == cols[q] - 2 * t, 1.0, 0.0).astype(BF)
            term = doubled[q] * mask[None]
            total = term if total is None else total + term
        tiles.append(total.reshape(width, 2 * width))
    return tiles


def send_kernel(pcol_hbm, up_hbm, down_hbm, par, p_hbm, out_a, out_b, pcol, up, down, p_v, sems, *, coarse):
    width = p_v.shape[1]
    copies = [
        pltpu.make_async_copy(source, target, sems.at[n])
        for n, (source, target) in enumerate(
            ((pcol_hbm, pcol), (up_hbm, up), (down_hbm, down), (p_hbm, p_v)))
    ]
    for copy in copies:
        copy.start()
    half = half_of_lane()
    even = par[0] == 0
    for copy in copies:
        copy.wait()
    for i in range(up.shape[0]):
        for out, first, second in ((out_b, down, up), (out_a, up, down)):
            f = jnp.where(even, first[i], second[i])
            cols = [pcol[q, f] for q in range(pcol.shape[0])]
            tiles = dense_row(p_v[f], cols, half, coarse)
            for t, tile in enumerate(tiles):
                out[i * width : (i + 1) * width, t * 128 : (t + 1) * 128] = tile


def own_kernel(acol, pcol, rcol, a_v, p_v, r_v, v_ref, ap_out, rd_out, spread_out, named, table, *, coarse):
    rows, width = a_v.shape[0], a_v.shape[1]
    kas, krs = acol.shape[0], rcol.shape[0]
    ghosts = rows // 4
    half = half_of_lane()
    table[rows * width :, :] = jnp.zeros((width, coarse * width), BF)

    def densify(f, _):
        cols = [pcol[q, f] for q in range(pcol.shape[0])]
        at = pl.ds(pl.multiple_of(f * width, width), width)
        for t, tile in enumerate(dense_row(p_v[f], cols, half, coarse)):
            table[at, t * 128 : (t + 1) * 128] = tile
        return 0

    lax.fori_loop(0, rows, densify, 0, unroll=4)

    def apply(f, count):
        picked = []
        sides = [jnp.int32(0), jnp.int32(0)]
        for k in range(kas):
            c = acol[k, f]
            if k > 0:
                sides[0] = jnp.where((c >= rows) & (c < rows + ghosts), 1, sides[0])
                sides[1] = jnp.where(c >= rows + ghosts, 1, sides[1])
            c = jnp.where(c < rows, c, rows)
            picked.append(table[pl.ds(pl.multiple_of(c * width, width), width), :])
        strip = jnp.dot(a_v[f], jnp.concatenate(picked, 0), preferred_element_type=F32)
        ap_out[pl.ds(pl.multiple_of(f * width, width), width), :] = strip.astype(BF)
        for side in (0, 1):
            named[count] = f + 64 * side
            count = count + sides[side]
        return count

    named[127] = lax.fori_loop(0, rows, apply, jnp.int32(0), unroll=8)

    right = lax.broadcasted_iota(jnp.int32, (width, 128), 1) >= width
    for pair in range(rows // 2):
        lanes = slice(pair * 128, (pair + 1) * 128)
        one, other = r_v[2 * pair], r_v[2 * pair + 1]
        blocks, names = [], []
        for j in range(krs):
            cut = slice(j * width, (j + 1) * width)
            blocks.append(jnp.concatenate([one[:, cut], other[:, cut]], 1))
            names.append(jnp.where(right, rcol[j, 2 * pair + 1], rcol[j, 2 * pair]).astype(F32).astype(BF))
        for s in range(3 * coarse):
            total = None
            for block, name in zip(blocks, names):
                term = jnp.where(name == jnp.asarray(s, BF), block, jnp.zeros_like(block))
                total = term if total is None else total + term
            rd_out[s * width : (s + 1) * width, lanes] = total

    flat = jnp.concatenate([v_ref[...].astype(F32), jnp.zeros((128 - rows, 2 * width), F32)], 0)
    turned = flat.T
    lane = lax.broadcasted_iota(jnp.int32, (width, 128), 1)
    both = jnp.where(lane < width, turned[:width], pltpu.roll(turned[width:], width, 1))
    at_lane = lane % width
    for f in range(rows):
        spread_out[f * width : (f + 1) * width, :] = jnp.where(at_lane == f, both, 0.0).astype(BF)


def spread_sums(spread, seg, width):
    pieces = []
    for n in range(seg // 128):
        t = spread[n * 128 : (n + 1) * 128].T
        pieces.append(jnp.concatenate(
            [jnp.sum(t[i * width : (i + 1) * width], 0, keepdims=True) for i in range(2)], 0))
    vec = jnp.concatenate(pieces, 1)
    return jnp.concatenate([vec, jnp.zeros((14, seg), F32)], 0)


def ghost_kernel(
    acol, named, par, got_a, got_b, a_v, rd_ref, ap_ref, spread_ref, send_a, send_b, own, own_vec,
    strips, pieces, table, *, coarse
):
    rows, width = a_v.shape[0], a_v.shape[1]
    kas = acol.shape[0]
    ghosts = got_a.shape[0] // width
    seg = coarse * width
    block = ghosts * width
    odd = par[0]
    table[pl.ds(pl.multiple_of((1 - odd) * block, block), block), :] = got_a[...]
    table[pl.ds(pl.multiple_of(odd * block, block), block), :] = got_b[...]
    table[2 * block :, :] = jnp.zeros((width, seg), BF)
    strips[...] = jnp.zeros_like(strips)
    count = named[127]
    batch = 6

    def apply(n, _):
        for i in range(batch):
            at = n * batch + i
            code = named[jnp.minimum(at, 126)]
            valid = at < count
            side = jnp.where(valid, code // 64, 0)
            f = jnp.where(valid, code % 64, 0)
            picked = []
            for k in range(kas):
                c = acol[k, f] - rows - side * ghosts
                c = jnp.where((c >= 0) & (c < ghosts), c + side * ghosts, 2 * ghosts)
                picked.append(table[pl.ds(pl.multiple_of(c * width, width), width), :])
            strip = jnp.dot(a_v[f], jnp.concatenate(picked, 0), preferred_element_type=F32)
            into = jnp.where(valid, f, rows)
            strips[side, pl.ds(pl.multiple_of(into * width, width), width), :] = strip.astype(BF)
        return 0

    lax.fori_loop(0, (count + batch - 1) // batch, apply, 0)
    deep = rows * width
    parts = (strips[0, 0:deep], ap_ref[...], strips[1, 0:deep])
    for e, part in enumerate(parts):
        lanes = slice(e * seg, (e + 1) * seg)
        for h in HS:
            sums = jnp.dot(rd_ref[h], part, preferred_element_type=F32)
            for n in range(sums.shape[0] // seg):
                at = h.start // seg + n
                block_sums = sums[n * seg : (n + 1) * seg]
                if at == 1:
                    own[:, lanes] = block_sums
                else:
                    pieces[at // 2, 0:seg, lanes] = block_sums.astype(BF)
    sums = jnp.dot(rd_ref[...], spread_ref[...], preferred_element_type=F32)
    own_vec[...] = spread_sums(sums[seg : 2 * seg], seg, width)
    for n in range(2):
        pieces[n, seg:, 0:seg] = spread_sums(sums[2 * n * seg : (2 * n + 1) * seg], seg, width).astype(BF)
        pieces[n, seg:, seg:] = jnp.zeros((16, 2 * seg), BF)
    send_a[...] = pieces[1 - odd]
    send_b[...] = pieces[odd]


def sum_kernel(dest, par, comp, got_a, got_b, own, own_vec, *outs, coarse):
    seg = own.shape[0]
    width = seg // coarse
    odd = par[0] == 1
    owners = [dest[0, s] for s in range(coarse)]
    ranks = []
    for s in range(coarse):
        rank = jnp.int32(0)
        for earlier in range(s):
            rank = rank + (owners[earlier] == owners[s]).astype(jnp.int32)
        ranks.append(rank)
    away = [lax.rem(owners[s] - comp[0] + 4, 4) for s in range(coarse)]
    low_vec = jnp.where(odd, got_a[seg : seg + 16, 0:seg].astype(F32), got_b[seg : seg + 16, 0:seg].astype(F32))
    high_vec = jnp.where(odd, got_b[seg : seg + 16, 0:seg].astype(F32), got_a[seg : seg + 16, 0:seg].astype(F32))
    vec = own_vec[...] + low_vec + high_vec
    lines = []
    for s in range(coarse):
        lines.append(jnp.concatenate(
            [vec[0:1, s * width : (s + 1) * width], vec[1:2, s * width : (s + 1) * width]], 1))
    row = lax.broadcasted_iota(jnp.int32, (16, 128), 0)
    for distance, out in enumerate(outs):
        block = jnp.zeros((16, 128), F32)
        for s in range(coarse):
            hit = jnp.where(away[s] == distance, ranks[s], -1)
            block = block + jnp.where(row == hit, lines[s], 0.0)
        out[2 * width :, 0:128] = block.astype(BF)
        out[2 * width :, 128:] = jnp.zeros((16, 5 * seg - 128), BF)
        for k in range(2):
            source = jnp.int32(-1)
            for s in range(coarse):
                source = jnp.where((away[s] == distance) & (ranks[s] == k), s, source)
            into = slice(k * width, (k + 1) * width)

            def fill(below, above, out=out, into=into, source=source):
                at = pl.ds(pl.multiple_of(jnp.maximum(source, 0) * width, width), width)
                for u in range(5):
                    total = None
                    for ref, first in ((own, 1), (below, 0), (above, 2)):
                        e = u - first
                        if 0 <= e < 3:
                            term = ref[at, e * seg : (e + 1) * seg].astype(F32)
                            total = term if total is None else total + term
                    out[into, u * seg : (u + 1) * seg] = total.astype(BF)

            @pl.when((source >= 0) & odd)
            def _():
                fill(got_a, got_b)

            @pl.when((source >= 0) & jnp.logical_not(odd))
            def _():
                fill(got_b, got_a)

            @pl.when(source < 0)
            def _():
                out[into, :] = jnp.zeros((width, 5 * seg), BF)


def gather_kernel(comp, *refs):
    parts, matrix, vectors = refs[:4], refs[4], refs[5]
    width = matrix.shape[1]
    row = lax.broadcasted_iota(jnp.int32, (8, 128), 0)
    total = jnp.zeros((8, 128), F32)
    for distance, part in enumerate(parts):
        source = lax.rem(comp[0] - distance + 4, 4)
        for k in range(2):
            matrix[source * 2 + k] = part[k * width : (k + 1) * width, :]
            line = part[2 * width :, 0:128].astype(F32)[k : k + 1]
            total = total + jnp.where(row == source * 2 + k, line, 0.0)
    vectors[...] = total.astype(BF)


def exchange(block_a, block_b):
    n = lax.axis_size("mesh")
    within = [(i, i ^ 1) for i in range(n)]
    across = [(i, i + 1 if i % 2 else i - 1) for i in range(1, n - 1)]
    got_b = lax.ppermute(block_b, "mesh", across)
    got_a = lax.ppermute(block_a, "mesh", within)
    return got_a, got_b


def on_device(a_blocks, a_columns, p_blocks, p_columns, r_blocks, r_columns, sent_up, sent_down, vectors, coarse_dest):
    rows, width = a_blocks.shape[0], a_blocks.shape[1]
    ghosts = sent_up.shape[0]
    coarse = coarse_dest.shape[0]
    seg = coarse * width
    acol, pcol, rcol, dest = a_columns.T, p_columns.T, r_columns.T, coarse_dest.T
    par = (lax.axis_index("mesh") % 2).astype(jnp.int32).reshape(1)
    comp = lax.axis_index("comp").astype(jnp.int32).reshape(1)
    shape = jax.ShapeDtypeStruct
    out_a, out_b = pl.pallas_call(
        functools.partial(send_kernel, coarse=coarse),
        out_shape=[shape((ghosts * width, seg), BF)] * 2,
        in_specs=[ANY, ANY, ANY, SM, ANY],
        out_specs=[VM, VM],
        scratch_shapes=[
            pltpu.SMEM(pcol.shape, jnp.int32),
            pltpu.SMEM(sent_up.shape, jnp.int32),
            pltpu.SMEM(sent_down.shape, jnp.int32),
            pltpu.VMEM(p_blocks.shape, BF),
            pltpu.SemaphoreType.DMA((4,)),
        ],
        compiler_params=params(K1_MIB),
        cost_estimate=pl.CostEstimate(flops=K1_FLOPS, bytes_accessed=10**6, transcendentals=0),
        name="send_rows",
    )(pcol, sent_up, sent_down, par, p_blocks)
    got_a, got_b = exchange(out_a, out_b)
    strips, r_dense, spread, named = pl.pallas_call(
        functools.partial(own_kernel, coarse=coarse),
        out_shape=[
            shape((rows * width, seg), BF),
            shape((3 * seg, rows * width), BF),
            shape((rows * width, 128), BF),
            shape((128,), jnp.int32),
        ],
        in_specs=[SM, SM, SM, VM, VM, VM, VM],
        out_specs=[VM, VM, VM, SM],
        scratch_shapes=[pltpu.VMEM(((rows + 1) * width, seg), BF)],
        compiler_params=params(K2_MIB),
        cost_estimate=pl.CostEstimate(flops=4 * 10**9, bytes_accessed=20 * 10**6, transcendentals=0),
        name="own_columns",
    )(acol, pcol, rcol, a_blocks, p_blocks, r_blocks, vectors)
    send_a, send_b, own, own_vec = pl.pallas_call(
        functools.partial(ghost_kernel, coarse=coarse),
        out_shape=[shape((seg + 16, 3 * seg), BF)] * 2 + [shape((seg, 3 * seg), F32), shape((16, seg), F32)],
        in_specs=[SM, SM, SM, VM, VM, VM, VM, VM, VM],
        out_specs=[VM] * 4,
        scratch_shapes=[
            pltpu.VMEM((2, (rows + 1) * width, seg), BF),
            pltpu.VMEM((2, seg + 16, 3 * seg), BF),
            pltpu.VMEM(((2 * ghosts + 1) * width, seg), BF),
        ],
        compiler_params=params(K2_MIB),
        name="ghost_columns",
    )(acol, named, par, got_a, got_b, a_blocks, r_dense, strips, spread)
    from_a, from_b = exchange(send_a, send_b)
    outs = pl.pallas_call(
        functools.partial(sum_kernel, coarse=coarse),
        out_shape=[shape((2 * width + 16, 5 * seg), BF)] * 4,
        in_specs=[SM, SM, SM, VM, VM, VM, VM],
        out_specs=[VM] * 4,
        compiler_params=params(),
        name="sum_rows",
    )(dest, par, comp, from_a, from_b, own, own_vec)
    parts = [outs[0]]
    turned = {}
    for distance in (2, 1, 3):
        turned[distance] = lax.ppermute(outs[distance], "comp", [(i, (i + distance) % 4) for i in range(4)])
    return pl.pallas_call(
        gather_kernel,
        out_shape=[shape((8, width, 5 * seg), BF), shape((8, 2 * width), BF)],
        in_specs=[SM] + [VM] * 4,
        out_specs=[VM, VM],
        compiler_params=params(),
        name="into_slots",
    )(comp, outs[0], turned[1], turned[2], turned[3])


def solution(mesh):
    placed = (
        P(("mesh", "comp"), None, None),
        P(("mesh", "comp"), None),
        P(("mesh", "comp"), None, None),
        P(("mesh", "comp"), None),
        P(("mesh", "comp"), None, None),
        P(("mesh", "comp"), None),
        P(("mesh", "comp")),
        P(("mesh", "comp")),
        P(("mesh", "comp"), None),
        P(("mesh", "comp"), None),
    )
    return jax.shard_map(
        on_device,
        mesh=mesh,
        in_specs=placed,
        out_specs=(P(("mesh", "comp"), None, None), P(("mesh", "comp"), None)),
        check_vma=False,
    )
```

```python
import functools

import jax
import jax.numpy as jnp
from jax import lax
from jax.experimental import pallas as pl
from jax.experimental.pallas import tpu as pltpu
from jax.sharding import PartitionSpec as P

BF = jnp.bfloat16
F32 = jnp.float32
MIB = 1 << 20
K1_MIB = 54
K1_FLOPS = 20 * 10**9
K2_MIB = 24
STASH = 30
K3_FLOPS = 3 * 10**9
K4_FLOPS = 3 * 10**9


def params(mib=24):
    return pltpu.CompilerParams(vmem_limit_bytes=mib * MIB)


VM = pl.BlockSpec(memory_space=pltpu.VMEM)
SM = pl.BlockSpec(memory_space=pltpu.SMEM)
ANY = pl.BlockSpec(memory_space=pl.ANY)


def half_of_lane():
    return (lax.broadcasted_iota(jnp.int32, (16, 128), 1) >= 64).astype(jnp.int32)


def dense_row(x, cols, half, coarse):
    width = x.shape[0]
    tiles = []
    doubled = []
    for q in range(len(cols)):
        block = x[:, q * width : (q + 1) * width]
        doubled.append(jnp.concatenate([block, block], 1).reshape(width // 16, 16, 2 * width))
    for t in range(coarse // 2):
        total = None
        for q in range(len(cols)):
            mask = jnp.where(half == cols[q] - 2 * t, 1.0, 0.0).astype(BF)
            term = doubled[q] * mask[None]
            total = term if total is None else total + term
        tiles.append(total.reshape(width, 2 * width))
    return tiles


def send_kernel(pcol_hbm, up_hbm, down_hbm, par, p_hbm, out_a, out_b, pcol, up, down, p_v, sems, *, coarse):
    width = p_v.shape[1]
    pairs = [(pcol_hbm, pcol), (up_hbm, up), (down_hbm, down), (p_hbm, p_v)]
    copies = [pltpu.make_async_copy(source, target, sems.at[n]) for n, (source, target) in enumerate(pairs)]
    for copy in copies:
        copy.start()
    half = half_of_lane()
    even = par[0] == 0
    for copy in copies:
        copy.wait()
    for i in range(up.shape[0]):
        for out, first, second in ((out_b, down, up), (out_a, up, down)):
            f = jnp.where(even, first[i], second[i])
            cols = [pcol[q, f] for q in range(pcol.shape[0])]
            tiles = dense_row(p_v[f], cols, half, coarse)
            for t, tile in enumerate(tiles):
                out[i * width : (i + 1) * width, t * 128 : (t + 1) * 128] = tile


def own_kernel(acol, pcol, rcol, a_v, p_v, r_v, v_ref, ap_out, sides_out, home_out, spread_out, named, table, *, coarse):
    rows, width = a_v.shape[0], a_v.shape[1]
    kas, krs = acol.shape[0], rcol.shape[0]
    ghosts = rows // 4
    half = half_of_lane()
    table[rows * width :, :] = jnp.zeros((width, coarse * width), BF)

    def densify(f, _):
        cols = [pcol[q, f] for q in range(pcol.shape[0])]
        at = pl.ds(pl.multiple_of(f * width, width), width)
        for t, tile in enumerate(dense_row(p_v[f], cols, half, coarse)):
            table[at, t * 128 : (t + 1) * 128] = tile
        return 0

    lax.fori_loop(0, rows, densify, 0, unroll=4)

    def apply(f, count):
        picked = []
        sides = [jnp.int32(0), jnp.int32(0)]
        for k in range(kas):
            c = acol[k, f]
            if k > 0:
                sides[0] = jnp.where((c >= rows) & (c < rows + ghosts), 1, sides[0])
                sides[1] = jnp.where(c >= rows + ghosts, 1, sides[1])
            c = jnp.where(c < rows, c, rows)
            picked.append(table[pl.ds(pl.multiple_of(c * width, width), width), :])
        strip = jnp.dot(a_v[f], jnp.concatenate(picked, 0), preferred_element_type=F32)
        ap_out[pl.ds(pl.multiple_of(f * width, width), width), :] = strip.astype(BF)
        for side in (0, 1):
            named[count] = f + 64 * side
            count = count + sides[side]
        return count

    named[127] = lax.fori_loop(0, rows, apply, jnp.int32(0), unroll=8)

    right = lax.broadcasted_iota(jnp.int32, (width, 128), 1) >= width
    for pair in range(rows // 2):
        lanes = slice(pair * 128, (pair + 1) * 128)
        one, other = r_v[2 * pair], r_v[2 * pair + 1]
        blocks, names = [], []
        for j in range(krs):
            cut = slice(j * width, (j + 1) * width)
            blocks.append(jnp.concatenate([one[:, cut], other[:, cut]], 1))
            names.append(jnp.where(right, rcol[j, 2 * pair + 1], rcol[j, 2 * pair]).astype(F32).astype(BF))
        for s in range(3 * coarse):
            total = None
            for block, name in zip(blocks, names):
                term = jnp.where(name == jnp.asarray(s, BF), block, jnp.zeros_like(block))
                total = term if total is None else total + term
            h, row = s // coarse, s % coarse * width
            if h == 1:
                into = pair // 2 * coarse * width + row
                home_out[into : into + width, pair % 2 * 128 : (pair % 2 + 1) * 128] = total
            else:
                row = row + h // 2 * coarse * width
                sides_out[row : row + width, lanes] = total

    flat = jnp.concatenate([v_ref[...].astype(F32), jnp.zeros((128 - rows, 2 * width), F32)], 0)
    turned = flat.T
    lane = lax.broadcasted_iota(jnp.int32, (width, 128), 1)
    both = jnp.where(lane < width, turned[:width], pltpu.roll(turned[width:], width, 1))
    at_lane = lane % width
    for f in range(rows):
        spread_out[f * width : (f + 1) * width, :] = jnp.where(at_lane == f, both, 0.0).astype(BF)


def spread_sums(spread, seg, width):
    pieces = []
    for n in range(seg // 128):
        t = spread[n * 128 : (n + 1) * 128].T
        pieces.append(jnp.concatenate(
            [jnp.sum(t[i * width : (i + 1) * width], 0, keepdims=True) for i in range(2)], 0))
    vec = jnp.concatenate(pieces, 1)
    return jnp.concatenate([vec, jnp.zeros((14, seg), F32)], 0)


def ghost_kernel(
    acol, named, par, got_a, got_b, a_v, rd_ref, home_ref, ap_ref, spread_ref, send_a, send_b, stash, strips, table, sems, *, coarse
):
    rows, width = a_v.shape[0], a_v.shape[1]
    kas = acol.shape[0]
    ghosts = got_a.shape[0] // width
    seg = coarse * width
    block = ghosts * width
    deep = rows * width
    stored = [
        pltpu.make_async_copy(home_ref, stash.at[2, 0:deep], sems.at[0]),
        pltpu.make_async_copy(spread_ref, stash.at[3, 0:deep, 0:128], sems.at[1]),
    ]
    for copy in stored:
        copy.start()
    odd = par[0]
    table[pl.ds(pl.multiple_of((1 - odd) * block, block), block), :] = got_a[...]
    table[pl.ds(pl.multiple_of(odd * block, block), block), :] = got_b[...]
    table[2 * block :, :] = jnp.zeros((width, seg), BF)
    strips[...] = jnp.zeros_like(strips)
    count = named[127]
    batch = 6

    def apply(n, _):
        for i in range(batch):
            at = n * batch + i
            code = named[jnp.minimum(at, 126)]
            valid = at < count
            side = jnp.where(valid, code // 64, 0)
            f = jnp.where(valid, code % 64, 0)
            picked = []
            for k in range(kas):
                c = acol[k, f] - rows - side * ghosts
                c = jnp.where((c >= 0) & (c < ghosts), c + side * ghosts, 2 * ghosts)
                picked.append(table[pl.ds(pl.multiple_of(c * width, width), width), :])
            strip = jnp.dot(a_v[f], jnp.concatenate(picked, 0), preferred_element_type=F32)
            into = jnp.where(valid, f, rows)
            strips[side, pl.ds(pl.multiple_of(into * width, width), width), :] = strip.astype(BF)
        return 0

    lax.fori_loop(0, (count + batch - 1) // batch, apply, 0)
    keep = pltpu.make_async_copy(strips, stash.at[0:2], sems.at[2])
    keep.start()
    parts = (strips[0, 0:deep], ap_ref[...], strips[1, 0:deep], spread_ref[...])
    for start, send in ((odd, send_b), (1 - odd, send_a)):
        restrict(rd_ref[pl.ds(pl.multiple_of(start * seg, seg), seg), :], parts, send, None)
    for copy in stored + [keep]:
        copy.wait()


def home_kernel(stash, ap_ref, own, own_vec, rd_ref, spread_ref, strips, sems):
    seg = own.shape[0]
    deep = ap_ref.shape[0]
    pairs = (
        (stash.at[2, 0:deep], rd_ref), (stash.at[0:2], strips), (stash.at[3, 0:deep, 0:128], spread_ref))
    copies = [pltpu.make_async_copy(source, target, sems.at[n]) for n, (source, target) in enumerate(pairs)]
    for copy in copies:
        copy.start()
    for copy in copies:
        copy.wait()
    parts = (strips[0, 0:deep], ap_ref[...], strips[1, 0:deep], spread_ref[...])
    r = jnp.concatenate([rd_ref[n * seg : (n + 1) * seg, :] for n in range(deep // seg)], 1)
    restrict(r, parts, own, own_vec)


def restrict(r, parts, out, out_vec):
    seg = r.shape[0]
    for e in range(3):
        sums = jnp.dot(r, parts[e], preferred_element_type=F32)
        out[0:seg, e * seg : (e + 1) * seg] = sums.astype(out.dtype)
    vec = spread_sums(jnp.dot(r, parts[3], preferred_element_type=F32), seg, 64)
    if out_vec is None:
        out[seg : seg + 16, 0:seg] = vec.astype(out.dtype)
        out[seg : seg + 16, seg:] = jnp.zeros((16, 2 * seg), out.dtype)
    else:
        out_vec[...] = vec


def sum_kernel(dest, par, comp, got_a, got_b, own, own_vec, *outs, coarse):
    seg = own.shape[0]
    width = seg // coarse
    odd = par[0] == 1
    owners = [dest[0, s] for s in range(coarse)]
    ranks = []
    for s in range(coarse):
        rank = jnp.int32(0)
        for earlier in range(s):
            rank = rank + (owners[earlier] == owners[s]).astype(jnp.int32)
        ranks.append(rank)
    away = [lax.rem(owners[s] - comp[0] + 4, 4) for s in range(coarse)]
    low_vec = jnp.where(odd, got_a[seg : seg + 16, 0:seg].astype(F32), got_b[seg : seg + 16, 0:seg].astype(F32))
    high_vec = jnp.where(odd, got_b[seg : seg + 16, 0:seg].astype(F32), got_a[seg : seg + 16, 0:seg].astype(F32))
    vec = own_vec[...] + low_vec + high_vec
    lines = []
    for s in range(coarse):
        lines.append(jnp.concatenate(
            [vec[0:1, s * width : (s + 1) * width], vec[1:2, s * width : (s + 1) * width]], 1))
    row = lax.broadcasted_iota(jnp.int32, (16, 128), 0)
    for distance, out in enumerate(outs):
        block = jnp.zeros((16, 128), F32)
        for s in range(coarse):
            hit = jnp.where(away[s] == distance, ranks[s], -1)
            block = block + jnp.where(row == hit, lines[s], 0.0)
        out[0:16, 10 * seg :] = block.astype(BF)
        out[16:, 10 * seg :] = jnp.zeros((width - 16, 128), BF)
        for k in range(2):
            source = jnp.int32(-1)
            for s in range(coarse):
                source = jnp.where((away[s] == distance) & (ranks[s] == k), s, source)
            first_lane = k * 5 * seg

            def fill(below, above, out=out, first_lane=first_lane, source=source):
                at = pl.ds(pl.multiple_of(jnp.maximum(source, 0) * width, width), width)
                for u in range(5):
                    total = None
                    for ref, first in ((own, 1), (below, 0), (above, 2)):
                        e = u - first
                        if 0 <= e < 3:
                            term = ref[at, e * seg : (e + 1) * seg].astype(F32)
                            total = term if total is None else total + term
                    out[:, first_lane + u * seg : first_lane + (u + 1) * seg] = total.astype(BF)

            @pl.when((source >= 0) & odd)
            def _():
                fill(got_a, got_b)

            @pl.when((source >= 0) & jnp.logical_not(odd))
            def _():
                fill(got_b, got_a)

            @pl.when(source < 0)
            def _():
                out[:, first_lane : first_lane + 5 * seg] = jnp.zeros((width, 5 * seg), BF)


def gather_kernel(comp, *refs):
    parts, matrix, vectors = refs[:4], refs[4], refs[5]
    wide = matrix.shape[2]
    row = lax.broadcasted_iota(jnp.int32, (8, 128), 0)
    total = jnp.zeros((8, 128), F32)
    for distance, part in enumerate(parts):
        source = lax.rem(comp[0] - distance + 4, 4)
        lines = part[0:16, 2 * wide :].astype(F32)
        for k in range(2):
            matrix[source * 2 + k] = part[:, k * wide : (k + 1) * wide]
            total = total + jnp.where(row == source * 2 + k, lines[k : k + 1], 0.0)
    vectors[...] = total.astype(BF)


def across(block):
    n = lax.axis_size("mesh")
    return lax.ppermute(block, "mesh", [(i, i + 1 if i % 2 else i - 1) for i in range(1, n - 1)])


def within(block):
    n = lax.axis_size("mesh")
    return lax.ppermute(block, "mesh", [(i, i ^ 1) for i in range(n)])


def on_device(a_blocks, a_columns, p_blocks, p_columns, r_blocks, r_columns, sent_up, sent_down, vectors, coarse_dest):
    rows, width = a_blocks.shape[0], a_blocks.shape[1]
    ghosts = sent_up.shape[0]
    coarse = coarse_dest.shape[0]
    seg = coarse * width
    acol, pcol, rcol, dest = a_columns.T, p_columns.T, r_columns.T, coarse_dest.T
    par = (lax.axis_index("mesh") % 2).astype(jnp.int32).reshape(1)
    comp = lax.axis_index("comp").astype(jnp.int32).reshape(1)
    shape = jax.ShapeDtypeStruct
    out_a, out_b = pl.pallas_call(
        functools.partial(send_kernel, coarse=coarse),
        out_shape=[shape((ghosts * width, seg), BF)] * 2,
        in_specs=[ANY, ANY, ANY, SM, ANY],
        out_specs=[VM, VM],
        scratch_shapes=[
            pltpu.SMEM(pcol.shape, jnp.int32),
            pltpu.SMEM(sent_up.shape, jnp.int32),
            pltpu.SMEM(sent_down.shape, jnp.int32),
            pltpu.VMEM(p_blocks.shape, BF),
            pltpu.SemaphoreType.DMA((4,)),
        ],
        compiler_params=params(K1_MIB),
        cost_estimate=pl.CostEstimate(flops=K1_FLOPS, bytes_accessed=10**6, transcendentals=0),
        name="send_rows",
    )(pcol, sent_up, sent_down, par, p_blocks)
    got_b, got_a = across(out_b), within(out_a)
    strips, sides_dense, home_dense, spread, named = pl.pallas_call(
        functools.partial(own_kernel, coarse=coarse),
        out_shape=[
            shape((rows * width, seg), BF),
            shape((2 * seg, rows * width), BF),
            shape((rows * width, seg), BF),
            shape((rows * width, 128), BF),
            shape((128,), jnp.int32),
        ],
        in_specs=[SM, SM, SM, VM, VM, VM, VM],
        out_specs=[VM, VM, VM, VM, SM],
        scratch_shapes=[pltpu.VMEM(((rows + 1) * width, seg), BF)],
        compiler_params=params(K2_MIB),
        cost_estimate=pl.CostEstimate(flops=4 * 10**9, bytes_accessed=20 * 10**6, transcendentals=0),
        name="own_columns",
    )(acol, pcol, rcol, a_blocks, p_blocks, r_blocks, vectors)
    send_a, send_b, stash = pl.pallas_call(
        functools.partial(ghost_kernel, coarse=coarse),
        out_shape=[shape((seg + 16, 3 * seg), BF)] * 2 + [shape((STASH, (rows + 1) * width, seg), BF)],
        in_specs=[SM, SM, SM] + [VM] * 7,
        out_specs=[VM, VM, ANY],
        scratch_shapes=[
            pltpu.VMEM((2, (rows + 1) * width, seg), BF),
            pltpu.VMEM(((2 * ghosts + 1) * width, seg), BF),
            pltpu.SemaphoreType.DMA((3,)),
        ],
        compiler_params=params(K2_MIB),
        cost_estimate=pl.CostEstimate(flops=K3_FLOPS, bytes_accessed=10**6, transcendentals=0),
        name="ghost_columns",
    )(acol, named, par, got_a, got_b, a_blocks, sides_dense, home_dense, strips, spread)
    from_b, from_a = across(send_b), within(send_a)
    own, own_vec = pl.pallas_call(
        home_kernel,
        out_shape=[shape((seg, 3 * seg), F32), shape((16, seg), F32)],
        in_specs=[ANY, VM],
        out_specs=[VM] * 2,
        scratch_shapes=[
            pltpu.VMEM((rows * width, seg), BF),
            pltpu.VMEM((rows * width, 128), BF),
            pltpu.VMEM((2, (rows + 1) * width, seg), BF),
            pltpu.SemaphoreType.DMA((3,)),
        ],
        compiler_params=params(K2_MIB),
        cost_estimate=pl.CostEstimate(flops=K4_FLOPS, bytes_accessed=10**6, transcendentals=0),
        name="home_rows",
    )(stash, strips)
    outs = pl.pallas_call(
        functools.partial(sum_kernel, coarse=coarse),
        out_shape=[shape((width, 10 * seg + 128), BF)] * 4,
        in_specs=[SM, SM, SM, VM, VM, VM, VM],
        out_specs=[VM] * 4,
        compiler_params=params(),
        name="sum_rows",
    )(dest, par, comp, from_a, from_b, own, own_vec)
    parts = [outs[0]]
    turned = {}
    for distance in (2, 1, 3):
        turned[distance] = lax.ppermute(outs[distance], "comp", [(i, (i + distance) % 4) for i in range(4)])
    return pl.pallas_call(
        gather_kernel,
        out_shape=[shape((8, width, 5 * seg), BF), shape((8, 2 * width), BF)],
        in_specs=[SM] + [VM] * 4,
        out_specs=[VM, VM],
        compiler_params=params(),
        name="into_slots",
    )(comp, outs[0], turned[1], turned[2], turned[3])


def solution(mesh):
    placed = (
        P(("mesh", "comp"), None, None),
        P(("mesh", "comp"), None),
        P(("mesh", "comp"), None, None),
        P(("mesh", "comp"), None),
        P(("mesh", "comp"), None, None),
        P(("mesh", "comp"), None),
        P(("mesh", "comp")),
        P(("mesh", "comp")),
        P(("mesh", "comp"), None),
        P(("mesh", "comp"), None),
    )
    return jax.shard_map(
        on_device,
        mesh=mesh,
        in_specs=placed,
        out_specs=(P(("mesh", "comp"), None, None), P(("mesh", "comp"), None)),
        check_vma=False,
    )
```

```python
import functools

import jax
import jax.numpy as jnp
from jax import lax
from jax.experimental import pallas as pl
from jax.experimental.pallas import tpu as pltpu
from jax.sharding import PartitionSpec as P

BF = jnp.bfloat16
F32 = jnp.float32
MIB = 1 << 20
K1_MIB = 54
K1_FLOPS = 20 * 10**9
K2_MIB = 24
STASH = 30
K3_FLOPS = 3 * 10**9
K4_FLOPS = 3 * 10**9


def params(mib=24):
    return pltpu.CompilerParams(vmem_limit_bytes=mib * MIB)


VM = pl.BlockSpec(memory_space=pltpu.VMEM)
SM = pl.BlockSpec(memory_space=pltpu.SMEM)
ANY = pl.BlockSpec(memory_space=pl.ANY)


def half_of_lane():
    return (lax.broadcasted_iota(jnp.int32, (16, 128), 1) >= 64).astype(jnp.int32)


def dense_row(x, cols, half, coarse):
    width = x.shape[0]
    tiles = []
    doubled = []
    for q in range(len(cols)):
        block = x[:, q * width : (q + 1) * width]
        doubled.append(jnp.concatenate([block, block], 1).reshape(width // 16, 16, 2 * width))
    for t in range(coarse // 2):
        total = None
        for q in range(len(cols)):
            mask = jnp.where(half == cols[q] - 2 * t, 1.0, 0.0).astype(BF)
            term = doubled[q] * mask[None]
            total = term if total is None else total + term
        tiles.append(total.reshape(width, 2 * width))
    return tiles


def send_kernel(pcol_hbm, up_hbm, down_hbm, par, p_hbm, out_a, out_b, pcol, up, down, p_v, sems, *, coarse):
    width = p_v.shape[1]
    pairs = [(pcol_hbm, pcol), (up_hbm, up), (down_hbm, down), (p_hbm, p_v)]
    copies = [pltpu.make_async_copy(source, target, sems.at[n]) for n, (source, target) in enumerate(pairs)]
    for copy in copies:
        copy.start()
    half = half_of_lane()
    even = par[0] == 0
    for copy in copies:
        copy.wait()
    for i in range(up.shape[0]):
        for out, first, second in ((out_b, down, up), (out_a, up, down)):
            f = jnp.where(even, first[i], second[i])
            cols = [pcol[q, f] for q in range(pcol.shape[0])]
            tiles = dense_row(p_v[f], cols, half, coarse)
            for t, tile in enumerate(tiles):
                out[i * width : (i + 1) * width, t * 128 : (t + 1) * 128] = tile


def own_kernel(acol, pcol, rcol, a_v, p_v, r_v, v_ref, ap_out, sides_out, home_out, spread_out, mid_out, vec_out, named, table, *, coarse):
    rows, width = a_v.shape[0], a_v.shape[1]
    kas, krs = acol.shape[0], rcol.shape[0]
    ghosts = rows // 4
    half = half_of_lane()
    table[rows * width :, :] = jnp.zeros((width, coarse * width), BF)

    def densify(f, _):
        cols = [pcol[q, f] for q in range(pcol.shape[0])]
        at = pl.ds(pl.multiple_of(f * width, width), width)
        for t, tile in enumerate(dense_row(p_v[f], cols, half, coarse)):
            table[at, t * 128 : (t + 1) * 128] = tile
        return 0

    lax.fori_loop(0, rows, densify, 0, unroll=16)

    def apply(f, count):
        picked = []
        sides = [jnp.int32(0), jnp.int32(0)]
        for k in range(kas):
            c = acol[k, f]
            if k > 0:
                sides[0] = jnp.where((c >= rows) & (c < rows + ghosts), 1, sides[0])
                sides[1] = jnp.where(c >= rows + ghosts, 1, sides[1])
            c = jnp.where(c < rows, c, rows)
            picked.append(table[pl.ds(pl.multiple_of(c * width, width), width), :])
        strip = jnp.dot(a_v[f], jnp.concatenate(picked, 0), preferred_element_type=F32)
        ap_out[pl.ds(pl.multiple_of(f * width, width), width), :] = strip.astype(BF)
        for side in (0, 1):
            named[count] = f + 64 * side
            count = count + sides[side]
        return count

    named[127] = lax.fori_loop(0, rows, apply, jnp.int32(0), unroll=48)

    right = lax.broadcasted_iota(jnp.int32, (width, 128), 1) >= width
    for pair in range(rows // 2):
        lanes = slice(pair * 128, (pair + 1) * 128)
        one, other = r_v[2 * pair], r_v[2 * pair + 1]
        blocks, names = [], []
        for j in range(krs):
            cut = slice(j * width, (j + 1) * width)
            blocks.append(jnp.concatenate([one[:, cut], other[:, cut]], 1))
            names.append(jnp.where(right, rcol[j, 2 * pair + 1], rcol[j, 2 * pair]).astype(F32).astype(BF))
        for s in range(3 * coarse):
            total = None
            for block, name in zip(blocks, names):
                term = jnp.where(name == jnp.asarray(s, BF), block, jnp.zeros_like(block))
                total = term if total is None else total + term
            h, row = s // coarse, s % coarse * width
            if h == 1:
                into = pair // 2 * coarse * width + row
                home_out[into : into + width, pair % 2 * 128 : (pair % 2 + 1) * 128] = total
            else:
                row = row + h // 2 * coarse * width
                sides_out[row : row + width, lanes] = total

    flat = jnp.concatenate([v_ref[...].astype(F32), jnp.zeros((128 - rows, 2 * width), F32)], 0)
    turned = flat.T
    lane = lax.broadcasted_iota(jnp.int32, (width, 128), 1)
    both = jnp.where(lane < width, turned[:width], pltpu.roll(turned[width:], width, 1))
    at_lane = lane % width
    for f in range(rows):
        spread_out[f * width : (f + 1) * width, :] = jnp.where(at_lane == f, both, 0.0).astype(BF)

    seg = coarse * width
    for side in (0, 1):
        at = slice(side * seg, (side + 1) * seg)
        r = sides_out[at, :]
        mid_out[at, :] = jnp.dot(r, ap_out[...], preferred_element_type=F32).astype(BF)
        sums = jnp.dot(r, spread_out[...], preferred_element_type=F32)
        vec_out[side * 16 : (side + 1) * 16, :] = spread_sums(sums, seg, width).astype(BF)


def spread_sums(spread, seg, width):
    pieces = []
    for n in range(seg // 128):
        t = spread[n * 128 : (n + 1) * 128].T
        pieces.append(jnp.concatenate(
            [jnp.sum(t[i * width : (i + 1) * width], 0, keepdims=True) for i in range(2)], 0))
    vec = jnp.concatenate(pieces, 1)
    return jnp.concatenate([vec, jnp.zeros((14, seg), F32)], 0)


def ghost_kernel(
    acol, named, par, got_a, got_b, a_v, rd_ref, home_ref, mid_ref, vec_ref, spread_ref, send_a, send_b, stash, strips, table, sems, *, coarse
):
    rows, width = a_v.shape[0], a_v.shape[1]
    kas = acol.shape[0]
    ghosts = got_a.shape[0] // width
    seg = coarse * width
    block = ghosts * width
    deep = rows * width
    stored = [
        pltpu.make_async_copy(home_ref, stash.at[2, 0:deep], sems.at[0]),
        pltpu.make_async_copy(spread_ref, stash.at[3, 0:deep, 0:128], sems.at[1]),
    ]
    for copy in stored:
        copy.start()
    odd = par[0]
    table[pl.ds(pl.multiple_of((1 - odd) * block, block), block), :] = got_a[...]
    table[pl.ds(pl.multiple_of(odd * block, block), block), :] = got_b[...]
    table[2 * block :, :] = jnp.zeros((width, seg), BF)
    strips[...] = jnp.zeros_like(strips)
    count = named[127]
    batch = 20

    def apply(n, _):
        for i in range(batch):
            at = n * batch + i
            code = named[jnp.minimum(at, 126)]
            valid = at < count
            side = jnp.where(valid, code // 64, 0)
            f = jnp.where(valid, code % 64, 0)
            picked = []
            for k in range(kas):
                c = acol[k, f] - rows - side * ghosts
                c = jnp.where((c >= 0) & (c < ghosts), c + side * ghosts, 2 * ghosts)
                picked.append(table[pl.ds(pl.multiple_of(c * width, width), width), :])
            strip = jnp.dot(a_v[f], jnp.concatenate(picked, 0), preferred_element_type=F32)
            into = jnp.where(valid, f, rows)
            strips[side, pl.ds(pl.multiple_of(into * width, width), width), :] = strip.astype(BF)
        return 0

    lax.fori_loop(0, (count + batch - 1) // batch, apply, 0)
    keep = pltpu.make_async_copy(strips, stash.at[0:2], sems.at[2])
    keep.start()
    for start, send in ((odd, send_b), (1 - odd, send_a)):
        at = pl.ds(pl.multiple_of(start * seg, seg), seg)
        r = rd_ref[at, :]
        for side in (0, 1):
            sums = jnp.dot(r, strips[side, 0:deep], preferred_element_type=F32)
            send[0:seg, 2 * side * seg : (2 * side + 1) * seg] = sums.astype(BF)
        send[0:seg, seg : 2 * seg] = mid_ref[at, :]
        send[seg:, 0:seg] = vec_ref[pl.ds(pl.multiple_of(start * 16, 16), 16), :]
        send[seg:, seg:] = jnp.zeros((16, 2 * seg), BF)
    for copy in stored + [keep]:
        copy.wait()


def home_kernel(stash, ap_ref, own, own_vec, rd_ref, spread_ref, strips, sems):
    seg = own.shape[0]
    deep = ap_ref.shape[0]
    pairs = (
        (stash.at[2, 0:deep], rd_ref), (stash.at[0:2], strips), (stash.at[3, 0:deep, 0:128], spread_ref))
    copies = [pltpu.make_async_copy(source, target, sems.at[n]) for n, (source, target) in enumerate(pairs)]
    for copy in copies:
        copy.start()
    for copy in copies:
        copy.wait()
    parts = (strips[0, 0:deep], ap_ref[...], strips[1, 0:deep], spread_ref[...])
    r = jnp.concatenate([rd_ref[n * seg : (n + 1) * seg, :] for n in range(deep // seg)], 1)
    restrict(r, parts, own, own_vec)


def restrict(r, parts, out, out_vec):
    seg = r.shape[0]
    for e in range(3):
        sums = jnp.dot(r, parts[e], preferred_element_type=F32)
        out[0:seg, e * seg : (e + 1) * seg] = sums.astype(out.dtype)
    vec = spread_sums(jnp.dot(r, parts[3], preferred_element_type=F32), seg, 64)
    out_vec[...] = vec


def sum_kernel(dest, par, comp, got_a, got_b, own, own_vec, *outs, coarse):
    seg = own.shape[0]
    width = seg // coarse
    odd = par[0] == 1
    owners = [dest[0, s] for s in range(coarse)]
    ranks = []
    for s in range(coarse):
        rank = jnp.int32(0)
        for earlier in range(s):
            rank = rank + (owners[earlier] == owners[s]).astype(jnp.int32)
        ranks.append(rank)
    away = [lax.rem(owners[s] - comp[0] + 4, 4) for s in range(coarse)]
    low_vec = jnp.where(odd, got_a[seg : seg + 16, 0:seg].astype(F32), got_b[seg : seg + 16, 0:seg].astype(F32))
    high_vec = jnp.where(odd, got_b[seg : seg + 16, 0:seg].astype(F32), got_a[seg : seg + 16, 0:seg].astype(F32))
    vec = own_vec[...] + low_vec + high_vec
    lines = []
    for s in range(coarse):
        lines.append(jnp.concatenate(
            [vec[0:1, s * width : (s + 1) * width], vec[1:2, s * width : (s + 1) * width]], 1))
    row = lax.broadcasted_iota(jnp.int32, (16, 128), 0)
    for distance, out in enumerate(outs):
        block = jnp.zeros((16, 128), F32)
        for s in range(coarse):
            hit = jnp.where(away[s] == distance, ranks[s], -1)
            block = block + jnp.where(row == hit, lines[s], 0.0)
        out[0:16, 10 * seg :] = block.astype(BF)
        out[16:, 10 * seg :] = jnp.zeros((width - 16, 128), BF)
        for k in range(2):
            source = jnp.int32(-1)
            for s in range(coarse):
                source = jnp.where((away[s] == distance) & (ranks[s] == k), s, source)
            first_lane = k * 5 * seg

            def fill(below, above, out=out, first_lane=first_lane, source=source):
                at = pl.ds(pl.multiple_of(jnp.maximum(source, 0) * width, width), width)
                for u in range(5):
                    total = None
                    for ref, first in ((own, 1), (below, 0), (above, 2)):
                        e = u - first
                        if 0 <= e < 3:
                            term = ref[at, e * seg : (e + 1) * seg].astype(F32)
                            total = term if total is None else total + term
                    out[:, first_lane + u * seg : first_lane + (u + 1) * seg] = total.astype(BF)

            @pl.when((source >= 0) & odd)
            def _():
                fill(got_a, got_b)

            @pl.when((source >= 0) & jnp.logical_not(odd))
            def _():
                fill(got_b, got_a)

            @pl.when(source < 0)
            def _():
                out[:, first_lane : first_lane + 5 * seg] = jnp.zeros((width, 5 * seg), BF)


def gather_kernel(comp, *refs):
    parts, matrix, vectors = refs[:4], refs[4], refs[5]
    wide = matrix.shape[2]
    row = lax.broadcasted_iota(jnp.int32, (8, 128), 0)
    total = jnp.zeros((8, 128), F32)
    for distance, part in enumerate(parts):
        source = lax.rem(comp[0] - distance + 4, 4)
        lines = part[0:16, 2 * wide :].astype(F32)
        for k in range(2):
            matrix[source * 2 + k] = part[:, k * wide : (k + 1) * wide]
            total = total + jnp.where(row == source * 2 + k, lines[k : k + 1], 0.0)
    vectors[...] = total.astype(BF)


def across(block):
    n = lax.axis_size("mesh")
    return lax.ppermute(block, "mesh", [(i, i + 1 if i % 2 else i - 1) for i in range(1, n - 1)])


def within(block):
    n = lax.axis_size("mesh")
    return lax.ppermute(block, "mesh", [(i, i ^ 1) for i in range(n)])


def on_device(a_blocks, a_columns, p_blocks, p_columns, r_blocks, r_columns, sent_up, sent_down, vectors, coarse_dest):
    rows, width = a_blocks.shape[0], a_blocks.shape[1]
    ghosts = sent_up.shape[0]
    coarse = coarse_dest.shape[0]
    seg = coarse * width
    acol, pcol, rcol, dest = a_columns.T, p_columns.T, r_columns.T, coarse_dest.T
    par = (lax.axis_index("mesh") % 2).astype(jnp.int32).reshape(1)
    comp = lax.axis_index("comp").astype(jnp.int32).reshape(1)
    shape = jax.ShapeDtypeStruct
    out_a, out_b = pl.pallas_call(
        functools.partial(send_kernel, coarse=coarse),
        out_shape=[shape((ghosts * width, seg), BF)] * 2,
        in_specs=[ANY, ANY, ANY, SM, ANY],
        out_specs=[VM, VM],
        scratch_shapes=[
            pltpu.SMEM(pcol.shape, jnp.int32),
            pltpu.SMEM(sent_up.shape, jnp.int32),
            pltpu.SMEM(sent_down.shape, jnp.int32),
            pltpu.VMEM(p_blocks.shape, BF),
            pltpu.SemaphoreType.DMA((4,)),
        ],
        compiler_params=params(K1_MIB),
        cost_estimate=pl.CostEstimate(flops=K1_FLOPS, bytes_accessed=10**6, transcendentals=0),
        name="send_rows",
    )(pcol, sent_up, sent_down, par, p_blocks)
    got_b, got_a = across(out_b), within(out_a)
    strips, sides_dense, home_dense, spread, mid, side_vec, named = pl.pallas_call(
        functools.partial(own_kernel, coarse=coarse),
        out_shape=[
            shape((rows * width, seg), BF),
            shape((2 * seg, rows * width), BF),
            shape((rows * width, seg), BF),
            shape((rows * width, 128), BF),
            shape((2 * seg, seg), BF),
            shape((32, seg), BF),
            shape((128,), jnp.int32),
        ],
        in_specs=[SM, SM, SM, VM, VM, VM, VM],
        out_specs=[VM] * 6 + [SM],
        scratch_shapes=[pltpu.VMEM(((rows + 1) * width, seg), BF)],
        compiler_params=params(K2_MIB),
        cost_estimate=pl.CostEstimate(flops=4 * 10**9, bytes_accessed=20 * 10**6, transcendentals=0),
        name="own_columns",
    )(acol, pcol, rcol, a_blocks, p_blocks, r_blocks, vectors)
    send_a, send_b, stash = pl.pallas_call(
        functools.partial(ghost_kernel, coarse=coarse),
        out_shape=[shape((seg + 16, 3 * seg), BF)] * 2 + [shape((STASH, (rows + 1) * width, seg), BF)],
        in_specs=[SM, SM, SM] + [VM] * 8,
        out_specs=[VM, VM, ANY],
        scratch_shapes=[
            pltpu.VMEM((2, (rows + 1) * width, seg), BF),
            pltpu.VMEM(((2 * ghosts + 1) * width, seg), BF),
            pltpu.SemaphoreType.DMA((3,)),
        ],
        compiler_params=params(K2_MIB),
        cost_estimate=pl.CostEstimate(flops=K3_FLOPS, bytes_accessed=10**6, transcendentals=0),
        name="ghost_columns",
    )(acol, named, par, got_a, got_b, a_blocks, sides_dense, home_dense, mid, side_vec, spread)
    from_b, from_a = across(send_b), within(send_a)
    own, own_vec = pl.pallas_call(
        home_kernel,
        out_shape=[shape((seg, 3 * seg), F32), shape((16, seg), F32)],
        in_specs=[ANY, VM],
        out_specs=[VM] * 2,
        scratch_shapes=[
            pltpu.VMEM((rows * width, seg), BF),
            pltpu.VMEM((rows * width, 128), BF),
            pltpu.VMEM((2, (rows + 1) * width, seg), BF),
            pltpu.SemaphoreType.DMA((3,)),
        ],
        compiler_params=params(K2_MIB),
        cost_estimate=pl.CostEstimate(flops=K4_FLOPS, bytes_accessed=10**6, transcendentals=0),
        name="home_rows",
    )(stash, strips)
    outs = pl.pallas_call(
        functools.partial(sum_kernel, coarse=coarse),
        out_shape=[shape((width, 10 * seg + 128), BF)] * 4,
        in_specs=[SM, SM, SM, VM, VM, VM, VM],
        out_specs=[VM] * 4,
        compiler_params=params(),
        name="sum_rows",
    )(dest, par, comp, from_a, from_b, own, own_vec)
    parts = [outs[0]]
    turned = {}
    for distance in (2, 1, 3):
        turned[distance] = lax.ppermute(outs[distance], "comp", [(i, (i + distance) % 4) for i in range(4)])
    return pl.pallas_call(
        gather_kernel,
        out_shape=[shape((8, width, 5 * seg), BF), shape((8, 2 * width), BF)],
        in_specs=[SM] + [VM] * 4,
        out_specs=[VM, VM],
        compiler_params=params(),
        name="into_slots",
    )(comp, outs[0], turned[1], turned[2], turned[3])


def solution(mesh):
    placed = (
        P(("mesh", "comp"), None, None),
        P(("mesh", "comp"), None),
        P(("mesh", "comp"), None, None),
        P(("mesh", "comp"), None),
        P(("mesh", "comp"), None, None),
        P(("mesh", "comp"), None),
        P(("mesh", "comp")),
        P(("mesh", "comp")),
        P(("mesh", "comp"), None),
        P(("mesh", "comp"), None),
    )
    return jax.shard_map(
        on_device,
        mesh=mesh,
        in_specs=placed,
        out_specs=(P(("mesh", "comp"), None, None), P(("mesh", "comp"), None)),
        check_vma=False,
    )
```

```python
import functools

import jax
import jax.numpy as jnp
from jax import lax
from jax.experimental import pallas as pl
from jax.experimental.pallas import tpu as pltpu
from jax.sharding import PartitionSpec as P

BF = jnp.bfloat16
F32 = jnp.float32
MIB = 1 << 20
K1_MIB = 54
K1_FLOPS = 20 * 10**9
K2_MIB = 24
STASH = 30
ORDER = (0, 2, 1, 3)
K3_FLOPS = 3 * 10**9
K4_FLOPS = 3 * 10**9


def params(mib=24):
    return pltpu.CompilerParams(vmem_limit_bytes=mib * MIB)


VM = pl.BlockSpec(memory_space=pltpu.VMEM)
SM = pl.BlockSpec(memory_space=pltpu.SMEM)
ANY = pl.BlockSpec(memory_space=pl.ANY)


def half_of_lane():
    return (lax.broadcasted_iota(jnp.int32, (16, 128), 1) >= 64).astype(jnp.int32)


def dense_row(x, cols, half, coarse):
    width = x.shape[0]
    tiles = []
    doubled = []
    for q in range(len(cols)):
        block = x[:, q * width : (q + 1) * width]
        doubled.append(jnp.concatenate([block, block], 1).reshape(width // 16, 16, 2 * width))
    for t in range(coarse // 2):
        total = None
        for q in range(len(cols)):
            mask = jnp.where(half == cols[q] - 2 * t, 1.0, 0.0).astype(BF)
            term = doubled[q] * mask[None]
            total = term if total is None else total + term
        tiles.append(total.reshape(width, 2 * width))
    return tiles


def send_kernel(pcol_hbm, up_hbm, down_hbm, par, p_hbm, out_a, out_b, pcol, up, down, p_v, sems, *, coarse):
    width = p_v.shape[1]
    pairs = [(pcol_hbm, pcol), (up_hbm, up), (down_hbm, down), (p_hbm, p_v)]
    copies = [pltpu.make_async_copy(source, target, sems.at[n]) for n, (source, target) in enumerate(pairs)]
    for copy in copies:
        copy.start()
    half = half_of_lane()
    even = par[0] == 0
    for copy in copies:
        copy.wait()
    for i in range(up.shape[0]):
        for out, first, second in ((out_b, down, up), (out_a, up, down)):
            f = jnp.where(even, first[i], second[i])
            cols = [pcol[q, f] for q in range(pcol.shape[0])]
            tiles = dense_row(p_v[f], cols, half, coarse)
            for t, tile in enumerate(tiles):
                out[i * width : (i + 1) * width, t * 128 : (t + 1) * 128] = tile


def own_kernel(acol, pcol, rcol, a_v, p_v, r_v, v_ref, ap_out, sides_out, home_out, spread_out, mid_out, vec_out, named, table, *, coarse):
    rows, width = a_v.shape[0], a_v.shape[1]
    kas, krs = acol.shape[0], rcol.shape[0]
    ghosts = rows // 4
    half = half_of_lane()
    table[rows * width :, :] = jnp.zeros((width, coarse * width), BF)

    def densify(f, _):
        cols = [pcol[q, f] for q in range(pcol.shape[0])]
        at = pl.ds(pl.multiple_of(f * width, width), width)
        for t, tile in enumerate(dense_row(p_v[f], cols, half, coarse)):
            table[at, t * 128 : (t + 1) * 128] = tile
        return 0

    lax.fori_loop(0, rows, densify, 0, unroll=16)

    def apply(f, count):
        picked = []
        sides = [jnp.int32(0), jnp.int32(0)]
        for k in range(kas):
            c = acol[k, f]
            if k > 0:
                sides[0] = jnp.where((c >= rows) & (c < rows + ghosts), 1, sides[0])
                sides[1] = jnp.where(c >= rows + ghosts, 1, sides[1])
            c = jnp.where(c < rows, c, rows)
            picked.append(table[pl.ds(pl.multiple_of(c * width, width), width), :])
        strip = jnp.dot(a_v[f], jnp.concatenate(picked, 0), preferred_element_type=F32)
        ap_out[pl.ds(pl.multiple_of(f * width, width), width), :] = strip.astype(BF)
        for side in (0, 1):
            named[count] = f + 64 * side
            count = count + sides[side]
        return count

    named[127] = lax.fori_loop(0, rows, apply, jnp.int32(0), unroll=48)

    right = lax.broadcasted_iota(jnp.int32, (width, 128), 1) >= width
    for pair in range(rows // 2):
        lanes = slice(pair * 128, (pair + 1) * 128)
        one, other = r_v[2 * pair], r_v[2 * pair + 1]
        blocks, names = [], []
        for j in range(krs):
            cut = slice(j * width, (j + 1) * width)
            blocks.append(jnp.concatenate([one[:, cut], other[:, cut]], 1))
            names.append(jnp.where(right, rcol[j, 2 * pair + 1], rcol[j, 2 * pair]).astype(F32).astype(BF))
        for s in range(3 * coarse):
            total = None
            for block, name in zip(blocks, names):
                term = jnp.where(name == jnp.asarray(s, BF), block, jnp.zeros_like(block))
                total = term if total is None else total + term
            h, row = s // coarse, s % coarse * width
            if h == 1:
                into = pair // 2 * coarse * width + row
                home_out[into : into + width, pair % 2 * 128 : (pair % 2 + 1) * 128] = total
            else:
                row = row + h // 2 * coarse * width
                sides_out[row : row + width, lanes] = total

    flat = jnp.concatenate([v_ref[...].astype(F32), jnp.zeros((128 - rows, 2 * width), F32)], 0)
    turned = flat.T
    lane = lax.broadcasted_iota(jnp.int32, (width, 128), 1)
    both = jnp.where(lane < width, turned[:width], pltpu.roll(turned[width:], width, 1))
    at_lane = lane % width
    for f in range(rows):
        spread_out[f * width : (f + 1) * width, :] = jnp.where(at_lane == f, both, 0.0).astype(BF)

    seg = coarse * width
    for side in (0, 1):
        at = slice(side * seg, (side + 1) * seg)
        r = sides_out[at, :]
        mid_out[at, :] = jnp.dot(r, ap_out[...], preferred_element_type=F32).astype(BF)
        sums = jnp.dot(r, spread_out[...], preferred_element_type=F32)
        vec_out[side * 16 : (side + 1) * 16, :] = spread_sums(sums, seg, width).astype(BF)


def spread_sums(spread, seg, width):
    pieces = []
    for n in range(seg // 128):
        t = spread[n * 128 : (n + 1) * 128].T
        pieces.append(jnp.concatenate(
            [jnp.sum(t[i * width : (i + 1) * width], 0, keepdims=True) for i in range(2)], 0))
    vec = jnp.concatenate(pieces, 1)
    return jnp.concatenate([vec, jnp.zeros((14, seg), F32)], 0)


def ghost_kernel(
    acol, named, par, got_b, got_a, a_v, rd_ref, home_ref, mid_ref, vec_ref, spread_ref, send_a, send_b, stash, strips, table, sems, *, coarse
):
    rows, width = a_v.shape[0], a_v.shape[1]
    kas = acol.shape[0]
    ghosts = got_a.shape[0] // width
    seg = coarse * width
    block = ghosts * width
    deep = rows * width
    stored = [
        pltpu.make_async_copy(home_ref, stash.at[2, 0:deep], sems.at[0]),
        pltpu.make_async_copy(spread_ref, stash.at[3, 0:deep, 0:128], sems.at[1]),
    ]
    for copy in stored:
        copy.start()
    odd = par[0]
    table[pl.ds(pl.multiple_of((1 - odd) * block, block), block), :] = got_a[...]
    table[pl.ds(pl.multiple_of(odd * block, block), block), :] = got_b[...]
    table[2 * block :, :] = jnp.zeros((width, seg), BF)
    strips[...] = jnp.zeros_like(strips)
    count = named[127]
    batch = 20

    def apply(n, _):
        for i in range(batch):
            at = n * batch + i
            code = named[jnp.minimum(at, 126)]
            valid = at < count
            side = jnp.where(valid, code // 64, 0)
            f = jnp.where(valid, code % 64, 0)
            picked = []
            for k in range(kas):
                c = acol[k, f] - rows - side * ghosts
                c = jnp.where((c >= 0) & (c < ghosts), c + side * ghosts, 2 * ghosts)
                picked.append(table[pl.ds(pl.multiple_of(c * width, width), width), :])
            strip = jnp.dot(a_v[f], jnp.concatenate(picked, 0), preferred_element_type=F32)
            into = jnp.where(valid, f, rows)
            strips[side, pl.ds(pl.multiple_of(into * width, width), width), :] = strip.astype(BF)
        return 0

    lax.fori_loop(0, (count + batch - 1) // batch, apply, 0)
    keep = pltpu.make_async_copy(strips, stash.at[0:2], sems.at[2])
    keep.start()
    for start, send in ((odd, send_b), (1 - odd, send_a)):
        at = pl.ds(pl.multiple_of(start * seg, seg), seg)
        r = rd_ref[at, :]
        for side in (0, 1):
            sums = jnp.dot(r, strips[side, 0:deep], preferred_element_type=F32)
            send[0:seg, 2 * side * seg : (2 * side + 1) * seg] = sums.astype(BF)
        send[0:seg, seg : 2 * seg] = mid_ref[at, :]
        send[seg:, 0:seg] = vec_ref[pl.ds(pl.multiple_of(start * 16, 16), 16), :]
        send[seg:, seg:] = jnp.zeros((16, 2 * seg), BF)
    for copy in stored + [keep]:
        copy.wait()


def home_kernel(stash, ap_ref, own, own_vec, rd_ref, spread_ref, strips, sems):
    seg = own.shape[0]
    deep = ap_ref.shape[0]
    pairs = (
        (stash.at[2, 0:deep], rd_ref), (stash.at[0:2], strips), (stash.at[3, 0:deep, 0:128], spread_ref))
    copies = [pltpu.make_async_copy(source, target, sems.at[n]) for n, (source, target) in enumerate(pairs)]
    for copy in copies:
        copy.start()
    for copy in copies:
        copy.wait()
    parts = (strips[0, 0:deep], ap_ref[...], strips[1, 0:deep], spread_ref[...])
    r = jnp.concatenate([rd_ref[n * seg : (n + 1) * seg, :] for n in range(deep // seg)], 1)
    restrict(r, parts, own, own_vec)


def restrict(r, parts, out, out_vec):
    seg = r.shape[0]
    for e in range(3):
        sums = jnp.dot(r, parts[e], preferred_element_type=F32)
        out[0:seg, e * seg : (e + 1) * seg] = sums.astype(out.dtype)
    vec = spread_sums(jnp.dot(r, parts[3], preferred_element_type=F32), seg, 64)
    out_vec[...] = vec


def sum_kernel(dest, par, comp, got_b, got_a, own, own_vec, *outs, coarse):
    seg = own.shape[0]
    width = seg // coarse
    odd = par[0] == 1
    owners = [dest[0, s] for s in range(coarse)]
    ranks = []
    for s in range(coarse):
        rank = jnp.int32(0)
        for earlier in range(s):
            rank = rank + (owners[earlier] == owners[s]).astype(jnp.int32)
        ranks.append(rank)
    away = [lax.rem(owners[s] - comp[0] + 4, 4) for s in range(coarse)]
    low_vec = jnp.where(odd, got_a[seg : seg + 16, 0:seg].astype(F32), got_b[seg : seg + 16, 0:seg].astype(F32))
    high_vec = jnp.where(odd, got_b[seg : seg + 16, 0:seg].astype(F32), got_a[seg : seg + 16, 0:seg].astype(F32))
    vec = own_vec[...] + low_vec + high_vec
    lines = []
    for s in range(coarse):
        lines.append(jnp.concatenate(
            [vec[0:1, s * width : (s + 1) * width], vec[1:2, s * width : (s + 1) * width]], 1))
    row = lax.broadcasted_iota(jnp.int32, (16, 128), 0)
    for distance, out in enumerate(outs):
        block = jnp.zeros((16, 128), F32)
        for s in range(coarse):
            hit = jnp.where(away[s] == distance, ranks[s], -1)
            block = block + jnp.where(row == hit, lines[s], 0.0)
        out[0:16, 10 * seg :] = block.astype(BF)
        out[16:, 10 * seg :] = jnp.zeros((width - 16, 128), BF)
        for k in range(2):
            source = jnp.int32(-1)
            for s in range(coarse):
                source = jnp.where((away[s] == distance) & (ranks[s] == k), s, source)
            first_lane = k * 5 * seg

            def fill(below, above, out=out, first_lane=first_lane, source=source):
                at = pl.ds(pl.multiple_of(jnp.maximum(source, 0) * width, width), width)
                for u in range(5):
                    total = None
                    for ref, first in ((own, 1), (below, 0), (above, 2)):
                        e = u - first
                        if 0 <= e < 3:
                            term = ref[at, e * seg : (e + 1) * seg].astype(F32)
                            total = term if total is None else total + term
                    out[:, first_lane + u * seg : first_lane + (u + 1) * seg] = total.astype(BF)

            @pl.when((source >= 0) & odd)
            def _():
                fill(got_a, got_b)

            @pl.when((source >= 0) & jnp.logical_not(odd))
            def _():
                fill(got_b, got_a)

            @pl.when(source < 0)
            def _():
                out[:, first_lane : first_lane + 5 * seg] = jnp.zeros((width, 5 * seg), BF)


def gather_kernel(comp, *refs):
    parts, matrix, vectors = refs[:4], refs[4], refs[5]
    wide = matrix.shape[2]
    row = lax.broadcasted_iota(jnp.int32, (8, 128), 0)
    total = jnp.zeros((8, 128), F32)
    for distance, part in zip(ORDER, parts):
        source = lax.rem(comp[0] - distance + 4, 4)
        lines = part[0:16, 2 * wide :].astype(F32)
        for k in range(2):
            matrix[source * 2 + k] = part[:, k * wide : (k + 1) * wide]
            total = total + jnp.where(row == source * 2 + k, lines[k : k + 1], 0.0)
    vectors[...] = total.astype(BF)


def across(block):
    n = lax.axis_size("mesh")
    return lax.ppermute(block, "mesh", [(i, i + 1 if i % 2 else i - 1) for i in range(1, n - 1)])


def within(block):
    n = lax.axis_size("mesh")
    return lax.ppermute(block, "mesh", [(i, i ^ 1) for i in range(n)])


def on_device(a_blocks, a_columns, p_blocks, p_columns, r_blocks, r_columns, sent_up, sent_down, vectors, coarse_dest):
    rows, width = a_blocks.shape[0], a_blocks.shape[1]
    ghosts = sent_up.shape[0]
    coarse = coarse_dest.shape[0]
    seg = coarse * width
    acol, pcol, rcol, dest = a_columns.T, p_columns.T, r_columns.T, coarse_dest.T
    par = (lax.axis_index("mesh") % 2).astype(jnp.int32).reshape(1)
    comp = lax.axis_index("comp").astype(jnp.int32).reshape(1)
    shape = jax.ShapeDtypeStruct
    out_a, out_b = pl.pallas_call(
        functools.partial(send_kernel, coarse=coarse),
        out_shape=[shape((ghosts * width, seg), BF)] * 2,
        in_specs=[ANY, ANY, ANY, SM, ANY],
        out_specs=[VM, VM],
        scratch_shapes=[
            pltpu.SMEM(pcol.shape, jnp.int32),
            pltpu.SMEM(sent_up.shape, jnp.int32),
            pltpu.SMEM(sent_down.shape, jnp.int32),
            pltpu.VMEM(p_blocks.shape, BF),
            pltpu.SemaphoreType.DMA((4,)),
        ],
        compiler_params=params(K1_MIB),
        cost_estimate=pl.CostEstimate(flops=K1_FLOPS, bytes_accessed=10**6, transcendentals=0),
        name="send_rows",
    )(pcol, sent_up, sent_down, par, p_blocks)
    got_b, got_a = across(out_b), within(out_a)
    strips, sides_dense, home_dense, spread, mid, side_vec, named = pl.pallas_call(
        functools.partial(own_kernel, coarse=coarse),
        out_shape=[
            shape((rows * width, seg), BF),
            shape((2 * seg, rows * width), BF),
            shape((rows * width, seg), BF),
            shape((rows * width, 128), BF),
            shape((2 * seg, seg), BF),
            shape((32, seg), BF),
            shape((128,), jnp.int32),
        ],
        in_specs=[SM, SM, SM, VM, VM, VM, VM],
        out_specs=[VM] * 6 + [SM],
        scratch_shapes=[pltpu.VMEM(((rows + 1) * width, seg), BF)],
        compiler_params=params(K2_MIB),
        cost_estimate=pl.CostEstimate(flops=4 * 10**9, bytes_accessed=20 * 10**6, transcendentals=0),
        name="own_columns",
    )(acol, pcol, rcol, a_blocks, p_blocks, r_blocks, vectors)
    send_a, send_b, stash = pl.pallas_call(
        functools.partial(ghost_kernel, coarse=coarse),
        out_shape=[shape((seg + 16, 3 * seg), BF)] * 2 + [shape((STASH, (rows + 1) * width, seg), BF)],
        in_specs=[SM, SM, SM] + [VM] * 8,
        out_specs=[VM, VM, ANY],
        scratch_shapes=[
            pltpu.VMEM((2, (rows + 1) * width, seg), BF),
            pltpu.VMEM(((2 * ghosts + 1) * width, seg), BF),
            pltpu.SemaphoreType.DMA((3,)),
        ],
        compiler_params=params(K2_MIB),
        cost_estimate=pl.CostEstimate(flops=K3_FLOPS, bytes_accessed=10**6, transcendentals=0),
        name="ghost_columns",
    )(acol, named, par, got_b, got_a, a_blocks, sides_dense, home_dense, mid, side_vec, spread)
    from_b, from_a = across(send_b), within(send_a)
    own, own_vec = pl.pallas_call(
        home_kernel,
        out_shape=[shape((seg, 3 * seg), F32), shape((16, seg), F32)],
        in_specs=[ANY, VM],
        out_specs=[VM] * 2,
        scratch_shapes=[
            pltpu.VMEM((rows * width, seg), BF),
            pltpu.VMEM((rows * width, 128), BF),
            pltpu.VMEM((2, (rows + 1) * width, seg), BF),
            pltpu.SemaphoreType.DMA((3,)),
        ],
        compiler_params=params(K2_MIB),
        cost_estimate=pl.CostEstimate(flops=K4_FLOPS, bytes_accessed=10**6, transcendentals=0),
        name="home_rows",
    )(stash, strips)
    outs = pl.pallas_call(
        functools.partial(sum_kernel, coarse=coarse),
        out_shape=[shape((width, 10 * seg + 128), BF)] * 4,
        in_specs=[SM, SM, SM, VM, VM, VM, VM],
        out_specs=[VM] * 4,
        compiler_params=params(),
        name="sum_rows",
    )(dest, par, comp, from_b, from_a, own, own_vec)
    parts = [outs[0]]
    turned = {}
    for distance in (2, 1, 3):
        turned[distance] = lax.ppermute(outs[distance], "comp", [(i, (i + distance) % 4) for i in range(4)])
    return pl.pallas_call(
        gather_kernel,
        out_shape=[shape((8, width, 5 * seg), BF), shape((8, 2 * width), BF)],
        in_specs=[SM] + [VM] * 4,
        out_specs=[VM, VM],
        compiler_params=params(),
        name="into_slots",
    )(comp, outs[0], *[turned[distance] for distance in ORDER[1:]])


def solution(mesh):
    placed = (
        P(("mesh", "comp"), None, None),
        P(("mesh", "comp"), None),
        P(("mesh", "comp"), None, None),
        P(("mesh", "comp"), None),
        P(("mesh", "comp"), None, None),
        P(("mesh", "comp"), None),
        P(("mesh", "comp")),
        P(("mesh", "comp")),
        P(("mesh", "comp"), None),
        P(("mesh", "comp"), None),
    )
    return jax.shard_map(
        on_device,
        mesh=mesh,
        in_specs=placed,
        out_specs=(P(("mesh", "comp"), None, None), P(("mesh", "comp"), None)),
        check_vma=False,
    )
```

```python
import functools

import jax
import jax.numpy as jnp
from jax import lax
from jax.experimental import pallas as pl
from jax.experimental.pallas import tpu as pltpu
from jax.sharding import PartitionSpec as P

BF = jnp.bfloat16
F32 = jnp.float32
MIB = 1 << 20
K1_MIB = 54
K1_FLOPS = 20 * 10**9
K2_MIB = 24
STASH = 30
ORDER = (0, 2, 1, 3)
K3_FLOPS = 3 * 10**9
K4_FLOPS = 3 * 10**9


def params(mib=24):
    return pltpu.CompilerParams(vmem_limit_bytes=mib * MIB)


VM = pl.BlockSpec(memory_space=pltpu.VMEM)
SM = pl.BlockSpec(memory_space=pltpu.SMEM)
ANY = pl.BlockSpec(memory_space=pl.ANY)


def half_of_lane():
    return (lax.broadcasted_iota(jnp.int32, (16, 128), 1) >= 64).astype(jnp.int32)


def dense_row(x, cols, half, coarse):
    width = x.shape[0]
    tiles = []
    doubled = []
    for q in range(len(cols)):
        block = x[:, q * width : (q + 1) * width]
        doubled.append(jnp.concatenate([block, block], 1).reshape(width // 16, 16, 2 * width))
    for t in range(coarse // 2):
        total = None
        for q in range(len(cols)):
            mask = jnp.where(half == cols[q] - 2 * t, 1.0, 0.0).astype(BF)
            term = doubled[q] * mask[None]
            total = term if total is None else total + term
        tiles.append(total.reshape(width, 2 * width))
    return tiles


def send_kernel(pcol_hbm, up_hbm, down_hbm, par, p_hbm, out_a, out_b, pcol, up, down, p_v, sems, *, coarse):
    width = p_v.shape[1]
    pairs = [(pcol_hbm, pcol), (up_hbm, up), (down_hbm, down), (p_hbm, p_v)]
    copies = [pltpu.make_async_copy(source, target, sems.at[n]) for n, (source, target) in enumerate(pairs)]
    for copy in copies:
        copy.start()
    half = half_of_lane()
    even = par[0] == 0
    for copy in copies:
        copy.wait()
    for i in range(up.shape[0]):
        for out, first, second in ((out_b, down, up), (out_a, up, down)):
            f = jnp.where(even, first[i], second[i])
            cols = [pcol[q, f] for q in range(pcol.shape[0])]
            tiles = dense_row(p_v[f], cols, half, coarse)
            for t, tile in enumerate(tiles):
                out[i * width : (i + 1) * width, t * 128 : (t + 1) * 128] = tile


def own_kernel(acol, pcol, rcol, a_v, p_v, r_v, v_ref, ap_out, sides_out, home_out, spread_out, mid_out, vec_out, named, table, *, coarse):
    rows, width = a_v.shape[0], a_v.shape[1]
    kas, krs = acol.shape[0], rcol.shape[0]
    ghosts = rows // 4
    half = half_of_lane()
    table[rows * width :, :] = jnp.zeros((width, coarse * width), BF)

    def densify(f, _):
        cols = [pcol[q, f] for q in range(pcol.shape[0])]
        at = pl.ds(pl.multiple_of(f * width, width), width)
        for t, tile in enumerate(dense_row(p_v[f], cols, half, coarse)):
            table[at, t * 128 : (t + 1) * 128] = tile
        return 0

    lax.fori_loop(0, rows, densify, 0, unroll=16)

    def apply(f, count):
        picked = []
        sides = [jnp.int32(0), jnp.int32(0)]
        for k in range(kas):
            c = acol[k, f]
            if k > 0:
                sides[0] = jnp.where((c >= rows) & (c < rows + ghosts), 1, sides[0])
                sides[1] = jnp.where(c >= rows + ghosts, 1, sides[1])
            c = jnp.where(c < rows, c, rows)
            picked.append(table[pl.ds(pl.multiple_of(c * width, width), width), :])
        strip = jnp.dot(a_v[f], jnp.concatenate(picked, 0), preferred_element_type=F32)
        ap_out[pl.ds(pl.multiple_of(f * width, width), width), :] = strip.astype(BF)
        for side in (0, 1):
            named[count] = f + 64 * side
            count = count + sides[side]
        return count

    named[127] = lax.fori_loop(0, rows, apply, jnp.int32(0), unroll=48)

    right = lax.broadcasted_iota(jnp.int32, (width, 128), 1) >= width
    for pair in range(rows // 2):
        lanes = slice(pair * 128, (pair + 1) * 128)
        one, other = r_v[2 * pair], r_v[2 * pair + 1]
        blocks, names = [], []
        for j in range(krs):
            cut = slice(j * width, (j + 1) * width)
            blocks.append(jnp.concatenate([one[:, cut], other[:, cut]], 1))
            names.append(jnp.where(right, rcol[j, 2 * pair + 1], rcol[j, 2 * pair]).astype(F32).astype(BF))
        for s in range(3 * coarse):
            total = None
            for block, name in zip(blocks, names):
                term = jnp.where(name == jnp.asarray(s, BF), block, jnp.zeros_like(block))
                total = term if total is None else total + term
            h, row = s // coarse, s % coarse * width
            if h == 1:
                into = pair // 2 * coarse * width + row
                home_out[into : into + width, pair % 2 * 128 : (pair % 2 + 1) * 128] = total
            else:
                row = row + h // 2 * coarse * width
                sides_out[row : row + width, lanes] = total

    flat = jnp.concatenate([v_ref[...].astype(F32), jnp.zeros((128 - rows, 2 * width), F32)], 0)
    turned = flat.T
    lane = lax.broadcasted_iota(jnp.int32, (width, 128), 1)
    both = jnp.where(lane < width, turned[:width], pltpu.roll(turned[width:], width, 1))
    at_lane = lane % width
    for f in range(rows):
        spread_out[f * width : (f + 1) * width, :] = jnp.where(at_lane == f, both, 0.0).astype(BF)

    seg = coarse * width
    for side in (0, 1):
        at = slice(side * seg, (side + 1) * seg)
        r = sides_out[at, :]
        mid_out[at, :] = jnp.dot(r, ap_out[...], preferred_element_type=F32).astype(BF)
        sums = jnp.dot(r, spread_out[...], preferred_element_type=F32)
        vec_out[side * 16 : (side + 1) * 16, :] = spread_sums(sums, seg, width).astype(BF)


def spread_sums(spread, seg, width):
    pieces = []
    for n in range(seg // 128):
        t = spread[n * 128 : (n + 1) * 128].T
        pieces.append(jnp.concatenate(
            [jnp.sum(t[i * width : (i + 1) * width], 0, keepdims=True) for i in range(2)], 0))
    vec = jnp.concatenate(pieces, 1)
    return jnp.concatenate([vec, jnp.zeros((14, seg), F32)], 0)


def ghost_kernel(
    acol, named, par, got_b, got_a, a_v, rd_ref, home_ref, mid_ref, vec_ref, spread_ref, send_a, send_b, stash, strips, table, sems, *, coarse
):
    rows, width = a_v.shape[0], a_v.shape[1]
    kas = acol.shape[0]
    ghosts = got_a.shape[0] // width
    seg = coarse * width
    block = ghosts * width
    deep = rows * width
    stored = [
        pltpu.make_async_copy(home_ref, stash.at[2, 0:deep], sems.at[0]),
        pltpu.make_async_copy(spread_ref, stash.at[3, 0:deep, 0:128], sems.at[1]),
    ]
    for copy in stored:
        copy.start()
    odd = par[0]
    table[pl.ds(pl.multiple_of((1 - odd) * block, block), block), :] = got_a[...]
    table[pl.ds(pl.multiple_of(odd * block, block), block), :] = got_b[...]
    table[2 * block :, :] = jnp.zeros((width, seg), BF)
    strips[...] = jnp.zeros_like(strips)
    count = named[127]
    batch = 26

    def apply(n, _):
        for i in range(batch):
            at = n * batch + i
            code = named[jnp.minimum(at, 126)]
            valid = at < count
            side = jnp.where(valid, code // 64, 0)
            f = jnp.where(valid, code % 64, 0)
            picked = []
            for k in range(kas):
                c = acol[k, f] - rows - side * ghosts
                c = jnp.where((c >= 0) & (c < ghosts), c + side * ghosts, 2 * ghosts)
                picked.append(table[pl.ds(pl.multiple_of(c * width, width), width), :])
            strip = jnp.dot(a_v[f], jnp.concatenate(picked, 0), preferred_element_type=F32)
            into = jnp.where(valid, f, rows)
            strips[side, pl.ds(pl.multiple_of(into * width, width), width), :] = strip.astype(BF)
        return 0

    lax.fori_loop(0, (count + batch - 1) // batch, apply, 0)
    keep = pltpu.make_async_copy(strips, stash.at[0:2], sems.at[2])
    keep.start()
    for start, send in ((odd, send_b), (1 - odd, send_a)):
        at = pl.ds(pl.multiple_of(start * seg, seg), seg)
        r = rd_ref[at, :]
        for side in (0, 1):
            sums = jnp.dot(r, strips[side, 0:deep], preferred_element_type=F32)
            send[0:seg, 2 * side * seg : (2 * side + 1) * seg] = sums.astype(BF)
        send[0:seg, seg : 2 * seg] = mid_ref[at, :]
        send[seg:, 0:seg] = vec_ref[pl.ds(pl.multiple_of(start * 16, 16), 16), :]
        send[seg:, seg:] = jnp.zeros((16, 2 * seg), BF)
    for copy in stored + [keep]:
        copy.wait()


def home_kernel(stash, ap_ref, own, own_vec, rd_ref, spread_ref, strips, sems):
    seg = own.shape[0]
    deep = ap_ref.shape[0]
    pairs = (
        (stash.at[2, 0:deep], rd_ref), (stash.at[0:2], strips), (stash.at[3, 0:deep, 0:128], spread_ref))
    copies = [pltpu.make_async_copy(source, target, sems.at[n]) for n, (source, target) in enumerate(pairs)]
    for copy in copies:
        copy.start()
    for copy in copies:
        copy.wait()
    parts = (strips[0, 0:deep], ap_ref[...], strips[1, 0:deep], spread_ref[...])
    r = jnp.concatenate([rd_ref[n * seg : (n + 1) * seg, :] for n in range(deep // seg)], 1)
    restrict(r, parts, own, own_vec)


def restrict(r, parts, out, out_vec):
    seg = r.shape[0]
    for e in range(3):
        sums = jnp.dot(r, parts[e], preferred_element_type=F32)
        out[0:seg, e * seg : (e + 1) * seg] = sums.astype(out.dtype)
    vec = spread_sums(jnp.dot(r, parts[3], preferred_element_type=F32), seg, 64)
    out_vec[...] = vec


def sum_kernel(dest, par, comp, got_b, got_a, own, own_vec, *outs, coarse):
    seg = own.shape[0]
    width = seg // coarse
    odd = par[0] == 1
    owners = [dest[0, s] for s in range(coarse)]
    ranks = []
    for s in range(coarse):
        rank = jnp.int32(0)
        for earlier in range(s):
            rank = rank + (owners[earlier] == owners[s]).astype(jnp.int32)
        ranks.append(rank)
    away = [lax.rem(owners[s] - comp[0] + 4, 4) for s in range(coarse)]
    low_vec = jnp.where(odd, got_a[seg : seg + 16, 0:seg].astype(F32), got_b[seg : seg + 16, 0:seg].astype(F32))
    high_vec = jnp.where(odd, got_b[seg : seg + 16, 0:seg].astype(F32), got_a[seg : seg + 16, 0:seg].astype(F32))
    vec = own_vec[...] + low_vec + high_vec
    lines = []
    for s in range(coarse):
        lines.append(jnp.concatenate(
            [vec[0:1, s * width : (s + 1) * width], vec[1:2, s * width : (s + 1) * width]], 1))
    row = lax.broadcasted_iota(jnp.int32, (16, 128), 0)
    for distance, out in enumerate(outs):
        block = jnp.zeros((16, 128), F32)
        for s in range(coarse):
            hit = jnp.where(away[s] == distance, ranks[s], -1)
            block = block + jnp.where(row == hit, lines[s], 0.0)
        out[0:16, 10 * seg :] = block.astype(BF)
        out[16:, 10 * seg :] = jnp.zeros((width - 16, 128), BF)
        for k in range(2):
            source = jnp.int32(-1)
            for s in range(coarse):
                source = jnp.where((away[s] == distance) & (ranks[s] == k), s, source)
            first_lane = k * 5 * seg

            def fill(below, above, out=out, first_lane=first_lane, source=source):
                at = pl.ds(pl.multiple_of(jnp.maximum(source, 0) * width, width), width)
                for u in range(5):
                    total = None
                    for ref, first in ((own, 1), (below, 0), (above, 2)):
                        e = u - first
                        if 0 <= e < 3:
                            term = ref[at, e * seg : (e + 1) * seg].astype(F32)
                            total = term if total is None else total + term
                    out[:, first_lane + u * seg : first_lane + (u + 1) * seg] = total.astype(BF)

            @pl.when((source >= 0) & odd)
            def _():
                fill(got_a, got_b)

            @pl.when((source >= 0) & jnp.logical_not(odd))
            def _():
                fill(got_b, got_a)

            @pl.when(source < 0)
            def _():
                out[:, first_lane : first_lane + 5 * seg] = jnp.zeros((width, 5 * seg), BF)


def gather_kernel(comp, *refs):
    parts, matrix, vectors = refs[:4], refs[4], refs[5]
    wide = matrix.shape[2]
    row = lax.broadcasted_iota(jnp.int32, (8, 128), 0)
    total = jnp.zeros((8, 128), F32)
    for distance, part in zip(ORDER, parts):
        source = lax.rem(comp[0] - distance + 4, 4)
        lines = part[0:16, 2 * wide :].astype(F32)
        for k in range(2):
            matrix[source * 2 + k] = part[:, k * wide : (k + 1) * wide]
            total = total + jnp.where(row == source * 2 + k, lines[k : k + 1], 0.0)
    vectors[...] = total.astype(BF)


def across(block):
    n = lax.axis_size("mesh")
    return lax.ppermute(block, "mesh", [(i, i + 1 if i % 2 else i - 1) for i in range(1, n - 1)])


def within(block):
    n = lax.axis_size("mesh")
    return lax.ppermute(block, "mesh", [(i, i ^ 1) for i in range(n)])


def on_device(a_blocks, a_columns, p_blocks, p_columns, r_blocks, r_columns, sent_up, sent_down, vectors, coarse_dest):
    rows, width = a_blocks.shape[0], a_blocks.shape[1]
    ghosts = sent_up.shape[0]
    coarse = coarse_dest.shape[0]
    seg = coarse * width
    acol, pcol, rcol, dest = a_columns.T, p_columns.T, r_columns.T, coarse_dest.T
    par = (lax.axis_index("mesh") % 2).astype(jnp.int32).reshape(1)
    comp = lax.axis_index("comp").astype(jnp.int32).reshape(1)
    shape = jax.ShapeDtypeStruct
    out_a, out_b = pl.pallas_call(
        functools.partial(send_kernel, coarse=coarse),
        out_shape=[shape((ghosts * width, seg), BF)] * 2,
        in_specs=[ANY, ANY, ANY, SM, ANY],
        out_specs=[VM, VM],
        scratch_shapes=[
            pltpu.SMEM(pcol.shape, jnp.int32),
            pltpu.SMEM(sent_up.shape, jnp.int32),
            pltpu.SMEM(sent_down.shape, jnp.int32),
            pltpu.VMEM(p_blocks.shape, BF),
            pltpu.SemaphoreType.DMA((4,)),
        ],
        compiler_params=params(K1_MIB),
        cost_estimate=pl.CostEstimate(flops=K1_FLOPS, bytes_accessed=10**6, transcendentals=0),
        name="send_rows",
    )(pcol, sent_up, sent_down, par, p_blocks)
    got_b, got_a = across(out_b), within(out_a)
    strips, sides_dense, home_dense, spread, mid, side_vec, named = pl.pallas_call(
        functools.partial(own_kernel, coarse=coarse),
        out_shape=[
            shape((rows * width, seg), BF),
            shape((2 * seg, rows * width), BF),
            shape((rows * width, seg), BF),
            shape((rows * width, 128), BF),
            shape((2 * seg, seg), BF),
            shape((32, seg), BF),
            shape((128,), jnp.int32),
        ],
        in_specs=[SM, SM, SM, VM, VM, VM, VM],
        out_specs=[VM] * 6 + [SM],
        scratch_shapes=[pltpu.VMEM(((rows + 1) * width, seg), BF)],
        compiler_params=params(K2_MIB),
        cost_estimate=pl.CostEstimate(flops=4 * 10**9, bytes_accessed=20 * 10**6, transcendentals=0),
        name="own_columns",
    )(acol, pcol, rcol, a_blocks, p_blocks, r_blocks, vectors)
    send_a, send_b, stash = pl.pallas_call(
        functools.partial(ghost_kernel, coarse=coarse),
        out_shape=[shape((seg + 16, 3 * seg), BF)] * 2 + [shape((STASH, (rows + 1) * width, seg), BF)],
        in_specs=[SM, SM, SM] + [VM] * 8,
        out_specs=[VM, VM, ANY],
        scratch_shapes=[
            pltpu.VMEM((2, (rows + 1) * width, seg), BF),
            pltpu.VMEM(((2 * ghosts + 1) * width, seg), BF),
            pltpu.SemaphoreType.DMA((3,)),
        ],
        compiler_params=params(K2_MIB),
        cost_estimate=pl.CostEstimate(flops=K3_FLOPS, bytes_accessed=10**6, transcendentals=0),
        name="ghost_columns",
    )(acol, named, par, got_b, got_a, a_blocks, sides_dense, home_dense, mid, side_vec, spread)
    from_b, from_a = across(send_b), within(send_a)
    own, own_vec = pl.pallas_call(
        home_kernel,
        out_shape=[shape((seg, 3 * seg), F32), shape((16, seg), F32)],
        in_specs=[ANY, VM],
        out_specs=[VM] * 2,
        scratch_shapes=[
            pltpu.VMEM((rows * width, seg), BF),
            pltpu.VMEM((rows * width, 128), BF),
            pltpu.VMEM((2, (rows + 1) * width, seg), BF),
            pltpu.SemaphoreType.DMA((3,)),
        ],
        compiler_params=params(K2_MIB),
        cost_estimate=pl.CostEstimate(flops=K4_FLOPS, bytes_accessed=10**6, transcendentals=0),
        name="home_rows",
    )(stash, strips)
    outs = pl.pallas_call(
        functools.partial(sum_kernel, coarse=coarse),
        out_shape=[shape((width, 10 * seg + 128), BF)] * 4,
        in_specs=[SM, SM, SM, VM, VM, VM, VM],
        out_specs=[VM] * 4,
        compiler_params=params(),
        name="sum_rows",
    )(dest, par, comp, from_b, from_a, own, own_vec)
    parts = [outs[0]]
    turned = {}
    for distance in (2, 1, 3):
        turned[distance] = lax.ppermute(outs[distance], "comp", [(i, (i + distance) % 4) for i in range(4)])
    return pl.pallas_call(
        gather_kernel,
        out_shape=[shape((8, width, 5 * seg), BF), shape((8, 2 * width), BF)],
        in_specs=[SM] + [VM] * 4,
        out_specs=[VM, VM],
        compiler_params=params(),
        name="into_slots",
    )(comp, outs[0], *[turned[distance] for distance in ORDER[1:]])


def solution(mesh):
    placed = (
        P(("mesh", "comp"), None, None),
        P(("mesh", "comp"), None),
        P(("mesh", "comp"), None, None),
        P(("mesh", "comp"), None),
        P(("mesh", "comp"), None, None),
        P(("mesh", "comp"), None),
        P(("mesh", "comp")),
        P(("mesh", "comp")),
        P(("mesh", "comp"), None),
        P(("mesh", "comp"), None),
    )
    return jax.shard_map(
        on_device,
        mesh=mesh,
        in_specs=placed,
        out_specs=(P(("mesh", "comp"), None, None), P(("mesh", "comp"), None)),
        check_vma=False,
    )
```
